256 devices in a mesh: space: 16 (over x_hi, z), filt: 16 (over y, x_lo, core).
Axes of the slice: x: 4 (x_hi: 2, x_lo: 2; x = x_hi * 2 + x_lo), y: 4, z: 8, core: 2. Of those that a mesh axis runs over, the one named last changes fastest.
Arguments:
- volume: bfloat16 [1, 256, 64, 16, 128], P(None, 'filt', 'space'), may hold values from -6 to 6
- weight: bfloat16 [3, 3, 3, 256, 256], P(None, None, None, 'filt'), may hold values from -0.078125 to 0.078125
- cotangent: bfloat16 [1, 256, 64, 16, 128], P(None, 'filt', 'space'), may hold values from -6 to 6
Outputs:
- activated: bfloat16 [1, 256, 64, 16, 128], P(None, 'filt', 'space')
- input_grad: bfloat16 [1, 256, 64, 16, 128], P(None, 'filt', 'space')
- weight_grad: float32 [3, 3, 3, 256, 256], P(None, None, None, 'filt', 'space')
The draws below stay inside these ranges and needn't reach their ends.
All inputs are finite; a program needn't handle non-finite values.
Results may differ from the reference program's by a relative error of at most 0.019.
Values may be sent and summed in bfloat16 or wider, within the bound.
No kernel may reach another device: no remote copies, remote signals or barrier semaphores. Data moves between devices by JAX's collectives and lax.ppermute only.
A program may use at most 128 MiB of HBM per device.

```python
import math
import jax
import jax.numpy as jnp
from jax import lax

CI = 256
CO = 256
B = 1
H = 16
W = 128
ND = 64


def block_levels(own_key, dims, shards, least, largest):
    def one(position, shards_of):
        steps = jax.random.uniform(jax.random.fold_in(jax.random.fold_in(own_key, 6), position), (shards_of,), jnp.float32, least / len(shards), largest / len(shards))
        return jnp.repeat(jnp.exp(steps), dims[position] // shards_of).reshape((-1,) + (1,) * (len(dims) - position - 1))

    level = one(*shards[0])
    for cut in shards[1:]:
        level = level * one(*cut)
    return level


def centred(key, shape, deviation, limit, cuts=(), dtype=jnp.bfloat16):
    array = jax.random.normal(key, shape, jnp.float32) * deviation
    if len(cuts) > 0:
        array = block_levels(key, shape, cuts, -0.22, 0.18) * array
    return jnp.clip(array, min=-limit, max=limit).astype(dtype)


def setup_inputs(seed: int = 0) -> dict:
    arg_keys = jax.random.split(jax.random.key(seed), 4)
    volume = centred(arg_keys[0], (B, CI, ND, H, W), 1.0, 6.0, ((1, 16), (2, 16)))
    weight = centred(arg_keys[1], (3, 3, 3, CO, CI), (27 * CI) ** -0.5, 0.078125, ((3, 16),))
    cotangent = centred(arg_keys[2], (B, CO, ND, H, W), 1.0, 6.0, ((1, 16), (2, 16)))
    return {"volume": volume, "weight": weight, "cotangent": cotangent}


def convolve(field, filters):
    return lax.conv_general_dilated(field, filters, (1, 1, 1), ((1, 1), (1, 1), (1, 1)), dimension_numbers=('NCDHW', 'OIDHW', 'NCDHW'), precision=lax.Precision.HIGHEST)

def reference(volume, weight, cotangent):
    field = volume.astype(jnp.float32)
    filters = jnp.transpose(weight, (3, 4, 0, 1, 2)).astype(jnp.float32)
    pre = convolve(field, filters)
    activated = jax.nn.silu(pre).astype(jnp.bfloat16)
    sigma = jax.nn.sigmoid(pre)
    pre_grad = (cotangent.astype(jnp.float32) * sigma * (1.0 + pre * (1.0 - sigma))).astype(jnp.bfloat16)
    _, pullback = jax.vjp(convolve, field, filters)
    field_grad, filter_grad = pullback(pre_grad.astype(jnp.float32))
    grad_scale = 1.0 / math.sqrt(B * ND * H * W)
    weight_grad = jnp.transpose(filter_grad, (2, 3, 4, 0, 1)) * grad_scale
    return (activated, field_grad.astype(jnp.bfloat16), weight_grad)
```

```python
import functools
import math

import jax
import jax.numpy as jnp
from jax import lax
from jax.experimental import pallas as pl
from jax.experimental.pallas import tpu as pltpu
from jax.sharding import Mesh, PartitionSpec as P

BREADTH = 128
GROUP = 4
VMEM_LIMIT = 40 * 1024 * 1024


def lane_shifted(value, by):
    if by == 0:
        return value
    lanes = value.shape[1]
    column = lax.broadcasted_iota(jnp.int32, value.shape, 1) % BREADTH
    moved = pltpu.roll(value, (-by) % lanes, 1)
    return jnp.where(column == (BREADTH - 1 if by > 0 else 0), 0.0, moved)


def row_shifted(value, by):
    if by == 0:
        return value
    gap = jnp.zeros((value.shape[0], BREADTH), value.dtype)
    if by > 0:
        return jnp.concatenate([value[:, BREADTH:], gap], axis=1)
    return jnp.concatenate([gap, value[:, :-BREADTH]], axis=1)


def folded(product, channels):
    total = None
    for c in range(3):
        column = None
        for b in range(3):
            at = (b * 3 + c) * channels
            part = row_shifted(product[at : at + channels], b - 1)
            column = part if column is None else column + part
        column = lane_shifted(column, c - 1)
        total = column if total is None else total + column
    return total


def partner(place_ref, axis, j):
    step = {"part": 1, "run": GROUP}[axis]
    return ((place_ref[0] // step) % GROUP) ^ j


def plane_of(space, part):
    return part ^ (part // 2) ^ ((space % 2) * (GROUP - 1))


def partner_plane(place_ref, j):
    return plane_of(place_ref[0] // GROUP**2, (place_ref[0] % GROUP) ^ j)


def at_end(place_ref, last):
    space, plane = place_ref[0] // GROUP**2, partner_plane(place_ref, 0)
    if last is None:
        return (space == 0) & (plane == 0)
    return (space == last) & (plane == GROUP - 1)


def unless(condition, value):
    return jnp.where(condition, jnp.zeros_like(value), value)


def block_rows(place_ref, axis, j, rows):
    return pl.ds(pl.multiple_of(partner(place_ref, axis, j) * rows, rows), rows)


def call(kernel, outputs, name, place, *operands, unread=(), scratch=()):
    def run(place_ref, *refs):
        kernel(place_ref, *refs[: len(operands)], *refs[len(operands) + len(unread) :])

    return pl.pallas_call(
        run,
        in_specs=[pl.BlockSpec(memory_space=pltpu.SMEM)]
        + [pl.BlockSpec(memory_space=pltpu.VMEM)] * len(operands)
        + [pl.BlockSpec(memory_space=pl.ANY)] * len(unread),
        out_specs=[pl.BlockSpec(memory_space=pltpu.VMEM)] * len(outputs),
        out_shape=[jax.ShapeDtypeStruct(shape, dtype) for shape, dtype in outputs],
        scratch_shapes=list(scratch),
        compiler_params=pltpu.CompilerParams(vmem_limit_bytes=VMEM_LIMIT),
        cost_estimate=pl.CostEstimate(flops=1, bytes_accessed=1, transcendentals=0),
        name=name,
    )(place, *operands, *unread)


def planes_kernel(place_ref, value_ref, out_ref):
    channels, planes, height, breadth = value_ref.shape
    for p in range(planes):
        value = value_ref[:, plane_of(place_ref[0] // GROUP**2, p)].astype(jnp.float32)
        out_ref[p] = value.reshape(channels, height * breadth).astype(out_ref.dtype)


def partner_planes_kernel(place_ref, value_ref, *outs):
    channels, _, height, breadth = value_ref.shape
    for j, out_ref in enumerate(outs):
        value = value_ref[:, partner_plane(place_ref, j)].astype(jnp.float32)
        out_ref[...] = value.reshape(channels, height * breadth).astype(out_ref.dtype)


def same_kernel(place_ref, value_ref, out_ref):
    del place_ref
    out_ref[...] = value_ref[...]


def halves_kernel(place_ref, value_ref, low_ref, high_ref):
    del place_ref
    half = low_ref.shape[0]
    low_ref[...] = value_ref[:half]
    high_ref[...] = value_ref[half:]


def edge_sums(place_ref, field_ref, matrices, out_ref, a):
    channels = out_ref.shape[0] // GROUP
    rows = 9 * channels
    for j, matrix_ref in enumerate(matrices):
        product = jnp.dot(
            matrix_ref[a * rows : (a + 1) * rows],
            field_ref[...],
            preferred_element_type=jnp.float32,
        )
        block = block_rows(place_ref, "part", j, channels)
        out_ref[block, :] = folded(product, channels).astype(out_ref.dtype)


def after_kernel(place_ref, *refs):
    halves, matrices = refs[: 2 * GROUP], refs[2 * GROUP : 3 * GROUP]
    field_ref, after_ref = refs[3 * GROUP :]
    for k, part_ref in enumerate(halves):
        half = part_ref.shape[0]
        start = partner(place_ref, "run", k // 2) * 2 * half + (k % 2) * half
        field_ref[pl.ds(pl.multiple_of(start, half), half), :] = part_ref[...]
    edge_sums(place_ref, field_ref, matrices, after_ref, 0)


def before_kernel(place_ref, field_ref, *refs):
    edge_sums(place_ref, field_ref, refs[:GROUP], refs[GROUP], 2)


def centre_kernel(place_ref, field_ref, *refs):
    edge_sums(place_ref, field_ref, refs[:GROUP], refs[GROUP], 1)


def gate_kernel(place_ref, same_ref, before_ref, after_ref, *refs, last):
    cotangents, active_ref, grad_ref = refs[:GROUP], refs[GROUP], refs[GROUP + 1]
    channels = cotangents[0].shape[0]
    for j, cotangent_ref in enumerate(cotangents):
        block = block_rows(place_ref, "part", j, channels)
        pre = (
            same_ref[block, :]
            + unless(at_end(place_ref, last), before_ref[block, :].astype(jnp.float32))
            + unless(at_end(place_ref, None), after_ref[block, :].astype(jnp.float32))
        )
        sigma = jax.nn.sigmoid(pre)
        active_ref[block, :] = (pre * sigma).astype(active_ref.dtype)
        grad_ref[block, :] = (
            cotangent_ref[...].astype(jnp.float32) * sigma * (1.0 + pre * (1.0 - sigma))
        ).astype(grad_ref.dtype)


def fill_moved(place_ref, moved_ref, grad_ref, low_ref, high_ref, last):
    plane = grad_ref.shape[1]
    stride = plane + 2 * BREADTH
    gap = jnp.zeros((grad_ref.shape[0], BREADTH), moved_ref.dtype)
    for p, ref in enumerate((low_ref, grad_ref, high_ref)):
        source = ref[...].astype(jnp.float32)
        if p != 1:
            source = unless(at_end(place_ref, last if p else None), source)
        for c in range(3):
            moved_ref[c, :, p * stride : p * stride + BREADTH] = gap
            moved_ref[c, :, p * stride + BREADTH : p * stride + BREADTH + plane] = lane_shifted(
                source, 1 - c
            ).astype(moved_ref.dtype)
            moved_ref[c, :, (p + 1) * stride - BREADTH : (p + 1) * stride] = gap


def tap_rows(moved_ref, block, plane):
    stride = plane + 2 * BREADTH
    parts = []
    for a in range(3):
        for b in range(3):
            for c in range(3):
                at = (2 - a) * stride + (2 - b) * BREADTH
                parts.append(moved_ref[c, block, at : at + plane])
    return jnp.concatenate(parts, axis=0)


def filter_kernel(place_ref, field_ref, grad_ref, low_ref, high_ref, *refs, last):
    outs, moved_ref = refs[:GROUP], refs[GROUP]
    rows, plane = grad_ref.shape
    fill_moved(place_ref, moved_ref, grad_ref, low_ref, high_ref, last)
    for j, out_ref in enumerate(outs):
        sums = lax.dot_general(
            field_ref[...],
            tap_rows(moved_ref, block_rows(place_ref, "part", j, rows // GROUP), plane),
            (((1,), (1,)), ((), ())),
            preferred_element_type=jnp.float32,
        )
        out_ref[...] = sums.astype(out_ref.dtype)


def input_kernel(place_ref, grad_ref, low_ref, high_ref, *refs, last):
    matrices, outs = refs[:GROUP], refs[GROUP : GROUP + 7]
    moved_ref, sum_ref = refs[GROUP + 7 :]
    rows, plane = grad_ref.shape
    fill_moved(place_ref, moved_ref, grad_ref, low_ref, high_ref, last)
    for j, matrix_ref in enumerate(matrices):
        part = lax.dot_general(
            matrix_ref[...],
            tap_rows(moved_ref, block_rows(place_ref, "part", j, rows // GROUP), plane),
            (((0,), (0,)), ((), ())),
            preferred_element_type=jnp.float32,
        )
        if j == 0:
            sum_ref[...] = part
        else:
            sum_ref[...] += part
    half = outs[1].shape[0]
    for out_ref, (j, start) in zip(outs, INPUT_CUTS):
        start = partner(place_ref, "run", j) * 2 * half + start * half
        block = pl.ds(pl.multiple_of(start, half), out_ref.shape[0])
        out_ref[...] = sum_ref[block, :].astype(out_ref.dtype)


INPUT_CUTS = ((0, 0), (2, 0), (2, 1), (1, 0), (3, 1), (1, 1), (3, 0))


def join_kernel(place_ref, near_ref, other_ref, high_ref, low_ref, near_out, other_out):
    del place_ref
    near_out[...] = (near_ref[...] + high_ref[...].astype(jnp.float32)).astype(near_out.dtype)
    other_out[...] = (other_ref[...] + low_ref[...].astype(jnp.float32)).astype(other_out.dtype)


def lift_kernel(place_ref, value_ref, other_ref, out_ref):
    del place_ref
    total = value_ref[...].astype(jnp.float32) + other_ref[...].astype(jnp.float32)
    out_ref[...] = total.astype(out_ref.dtype)


def merge_kernel(place_ref, *refs):
    del place_ref
    values, out_ref = refs[:-1], refs[-1]
    total = values[0][...].astype(jnp.float32)
    for ref in values[1:]:
        total += ref[...].astype(jnp.float32)
    out_ref[...] = total.astype(out_ref.dtype)


def pair_kernel(place_ref, own_ref, *refs):
    halves, active_ref, outs, sum_ref = refs[:4], refs[4], refs[5 : 5 + GROUP], refs[5 + GROUP]
    half = halves[0].shape[0]
    for k in range(2):
        rows = slice(k * half, (k + 1) * half)
        sum_ref[rows, :] = (
            own_ref[rows, :]
            + halves[k][...].astype(jnp.float32)
            + halves[2 + k][...].astype(jnp.float32)
        )
    for j, out_ref in enumerate(outs):
        block = block_rows(place_ref, "part", j, out_ref.shape[1])
        out_ref[0] = active_ref[block, :]
        out_ref[1] = sum_ref[block, :].astype(out_ref.dtype)


def close_kernel(place_ref, *refs):
    pairs, outs = refs[:GROUP], refs[GROUP:]
    for j, pair_ref in enumerate(pairs):
        for k, out_ref in enumerate(outs):
            channels, _, height, breadth = out_ref.shape
            value = pair_ref[k].astype(jnp.float32).reshape(channels, height, breadth)
            out_ref[:, partner_plane(place_ref, j)] = value.astype(out_ref.dtype)


def total_kernel(place_ref, parts_ref, out_ref, *, scale):
    del place_ref
    total = parts_ref[0].astype(jnp.float32)
    for s in range(1, parts_ref.shape[0]):
        total += parts_ref[s].astype(jnp.float32)
    out_ref[...] = jnp.transpose(total * scale)


DEPTH = ("space", "part")
CHANNELS = ("run", "part")


def shifted(value, by):
    count = lax.axis_size(DEPTH)
    at = {
        space * GROUP + plane_of(space, part): space * GROUP + part
        for space in range(count // GROUP)
        for part in range(GROUP)
    }
    return lax.ppermute(value, DEPTH, [(at[i], at[(i + by) % count]) for i in range(count)])


def swap(value, axis, j):
    return lax.ppermute(value, axis, [(i, i ^ j) for i in range(lax.axis_size(axis))])


def swapped(values, axis):
    return [values[0]] + [swap(values[j], axis, j) for j in range(1, GROUP)]


def body(volume, weight, cotangent):
    batch, in_local, planes, height, breadth = volume.shape
    out_local, in_total = weight.shape[3:]
    spaces = lax.axis_size("space")
    plane = height * breadth
    rows, depth, taps = GROUP * out_local, GROUP * in_local, 27 * out_local
    half = depth // 2
    grad_scale = 1.0 / math.sqrt(batch * planes * plane * spaces)
    bf16, f32 = jnp.bfloat16, jnp.float32
    place = lax.axis_index(("space", "run", "part")).reshape(1)
    ends = {"last": spaces - 1}

    (field,) = call(
        planes_kernel, [((planes, in_local, plane), bf16)], "volume_planes", place, volume[0]
    )
    field = lax.all_to_all(field, "part", split_axis=0, concat_axis=0, tiled=True)
    low, high = call(
        halves_kernel, [((half, plane), bf16)] * 2, "halves", place, field.reshape(depth, plane)
    )
    low_1, high_3 = swap(low, "run", 1), swap(high, "run", 3)
    high_1, low_3 = swap(high, "run", 1), swap(low, "run", 3)
    (matrix,) = call(
        same_kernel,
        [((taps, in_total), bf16)],
        "filters",
        place,
        weight.reshape(taps, in_total),
        unread=[low],
    )
    matrix_1, matrix_2 = swap(matrix, "part", 1), swap(matrix, "part", 2)
    low_2, high_2 = swap(low_1, "run", 3), swap(high_3, "run", 1)
    matrices = [matrix, matrix_1, matrix_2, swap(matrix_2, "part", 1)]
    cotangents = call(
        partner_planes_kernel,
        [((out_local, plane), bf16)] * GROUP,
        "cotangent_planes",
        place,
        cotangent[0],
        unread=[low_1, high_3],
    )
    cotangents = swapped(cotangents, "part")

    field, after = call(
        after_kernel,
        [((in_total, plane), bf16), ((rows, plane), bf16)],
        "after",
        place,
        *(low, high, low_1, high_1, low_2, high_2, low_3, high_3),
        *matrices,
    )
    after = shifted(after, 1)
    (before,) = call(
        before_kernel, [((rows, plane), bf16)], "before", place, field, *matrices
    )
    (same,) = call(
        centre_kernel,
        [((rows, plane), f32)],
        "centre",
        place,
        field,
        *matrices,
        unread=[before],
    )
    before = shifted(before, -1)
    active, grad = call(
        functools.partial(gate_kernel, **ends),
        [((rows, plane), bf16)] * 2,
        "gate",
        place,
        same,
        before,
        after,
        *cotangents,
    )

    around = (grad, shifted(grad, 1), shifted(grad, -1))
    moved = pltpu.VMEM((3, rows, 3 * (plane + 2 * BREADTH)), bf16)
    sums, sums_1, sums_2, sums_3 = call(
        functools.partial(filter_kernel, **ends),
        [((in_total, taps), bf16)] * GROUP,
        "filter_sums",
        place,
        field,
        *around,
        scratch=[moved],
    )
    sums_3, sums_1 = swap(sums_3, "part", 1), swap(sums_1, "part", 1)
    own, far_low, far_high, low_1, high_3, high_1, low_3 = call(
        functools.partial(input_kernel, **ends),
        [((depth, plane), f32)] + [((half, plane), bf16)] * 4 + [((half, plane), f32)] * 2,
        "input_sums",
        place,
        *around,
        *matrices,
        unread=[sums],
        scratch=[moved, pltpu.VMEM((in_total, plane), f32)],
    )
    far_low, far_high = swap(far_low, "run", 1), swap(far_high, "run", 3)
    low_1, high_3 = swap(low_1, "run", 1), swap(high_3, "run", 3)
    high_1, low_3 = call(
        join_kernel,
        [((half, plane), bf16)] * 2,
        "join",
        place,
        high_1,
        low_3,
        far_high,
        far_low,
    )
    high_1, low_3 = swap(high_1, "run", 1), swap(low_3, "run", 3)
    (sums_2,) = call(
        lift_kernel, [((in_total, taps), bf16)], "lift", place, sums_2, sums_3, unread=[far_low]
    )
    pairs = call(
        pair_kernel,
        [((2, in_local, plane), bf16)] * GROUP,
        "pairs",
        place,
        *(own, low_1, high_1, low_3, high_3),
        active,
        unread=[sums_2],
        scratch=[pltpu.VMEM((depth, plane), f32)],
    )
    sums_2 = swap(sums_2, "part", 2)
    pairs = swapped(pairs, "part")
    (sums,) = call(
        merge_kernel,
        [((in_total, taps), bf16)],
        "merge",
        place,
        *(sums, sums_1, sums_2),
        unread=[pairs[1]],
    )
    sums = lax.all_to_all(
        sums.reshape(spaces, in_total // spaces, taps),
        "space",
        split_axis=0,
        concat_axis=0,
        tiled=True,
    )
    (total,) = call(
        functools.partial(total_kernel, scale=grad_scale),
        [((taps, in_total // spaces), f32)],
        "total",
        place,
        sums,
    )
    active, back = call(
        close_kernel,
        [((in_local, planes, height, breadth), bf16)] * 2,
        "close",
        place,
        *pairs,
    )
    return (
        active[None],
        back[None],
        total.reshape(3, 3, 3, out_local, in_total // spaces),
    )


def solution(mesh):
    spaces, filts = mesh.devices.shape
    cut = Mesh(mesh.devices.reshape(spaces, filts // GROUP, GROUP), ("space", "run", "part"))
    in_specs = (
        P(None, CHANNELS, "space", None, None),
        P(None, None, None, CHANNELS, None),
        P(None, CHANNELS, "space", None, None),
    )
    out_specs = (
        P(None, CHANNELS, "space", None, None),
        P(None, CHANNELS, "space", None, None),
        P(None, None, None, CHANNELS, "space"),
    )
    return jax.shard_map(body, mesh=cut, in_specs=in_specs, out_specs=out_specs, check_vma=False)
```

```python
import functools
import math

import jax
import jax.numpy as jnp
from jax import lax
from jax.experimental import pallas as pl
from jax.experimental.pallas import tpu as pltpu
from jax.sharding import Mesh, PartitionSpec as P

BREADTH = 128
GROUP = 4
LAYERS = 8
VMEM_LIMIT = 40 * 1024 * 1024


def lane_shifted(value, by):
    if by == 0:
        return value
    lanes = value.shape[1]
    column = lax.broadcasted_iota(jnp.int32, value.shape, 1) % BREADTH
    moved = pltpu.roll(value, (-by) % lanes, 1)
    return jnp.where(column == (BREADTH - 1 if by > 0 else 0), 0.0, moved)


def row_shifted(value, by):
    if by == 0:
        return value
    gap = jnp.zeros((value.shape[0], BREADTH), value.dtype)
    if by > 0:
        return jnp.concatenate([value[:, BREADTH:], gap], axis=1)
    return jnp.concatenate([gap, value[:, :-BREADTH]], axis=1)


def folded(product, channels):
    total = None
    for c in range(3):
        column = None
        for b in range(3):
            at = (b * 3 + c) * channels
            part = row_shifted(product[at : at + channels], b - 1)
            column = part if column is None else column + part
        column = lane_shifted(column, c - 1)
        total = column if total is None else total + column
    return total


def partner(place_ref, axis, j):
    step = {"part": 1, "run": GROUP}[axis]
    return ((place_ref[0] // step) % GROUP) ^ j


def plane_of(space, part):
    backwards = (1 + space + space // LAYERS) % 2
    return part ^ (part // 2) ^ (backwards * (GROUP - 1))


def partner_plane(place_ref, j):
    return plane_of(place_ref[0] // GROUP**2, (place_ref[0] % GROUP) ^ j)


def at_end(place_ref, last):
    space, plane = place_ref[0] // GROUP**2, partner_plane(place_ref, 0)
    if last is None:
        return (space == 0) & (plane == 0)
    return (space == last) & (plane == GROUP - 1)


def unless(condition, value):
    return jnp.where(condition, jnp.zeros_like(value), value)


def block_rows(place_ref, axis, j, rows):
    return pl.ds(pl.multiple_of(partner(place_ref, axis, j) * rows, rows), rows)


def call(kernel, outputs, name, place, *operands, unread=(), scratch=()):
    def run(place_ref, *refs):
        kernel(place_ref, *refs[: len(operands)], *refs[len(operands) + len(unread) :])

    return pl.pallas_call(
        run,
        in_specs=[pl.BlockSpec(memory_space=pltpu.SMEM)]
        + [pl.BlockSpec(memory_space=pltpu.VMEM)] * len(operands)
        + [pl.BlockSpec(memory_space=pl.ANY)] * len(unread),
        out_specs=[pl.BlockSpec(memory_space=pltpu.VMEM)] * len(outputs),
        out_shape=[jax.ShapeDtypeStruct(shape, dtype) for shape, dtype in outputs],
        scratch_shapes=list(scratch),
        compiler_params=pltpu.CompilerParams(vmem_limit_bytes=VMEM_LIMIT),
        cost_estimate=pl.CostEstimate(flops=1, bytes_accessed=1, transcendentals=0),
        name=name,
    )(place, *operands, *unread)


def planes_kernel(place_ref, value_ref, *outs):
    channels, _, height, breadth = value_ref.shape
    for j, out_ref in enumerate(outs):
        value = value_ref[:, partner_plane(place_ref, j)].astype(jnp.float32)
        out_ref[...] = value.reshape(channels, height * breadth).astype(out_ref.dtype)


def rest_kernel(place_ref, cotangent_ref, filters_ref, matrix_ref, *outs):
    planes_kernel(place_ref, cotangent_ref, *outs)
    matrix_ref[...] = filters_ref[...]


def halves_kernel(place_ref, *refs):
    pieces, (low_ref, high_ref, order_ref) = refs[:GROUP], refs[GROUP:]
    half = low_ref.shape[0]
    for j, piece_ref in enumerate(pieces):
        order_ref[block_rows(place_ref, "part", j, half // 2), :] = piece_ref[...]
    low_ref[...] = order_ref[:half]
    high_ref[...] = order_ref[half:]


def edge_sums(place_ref, field_ref, matrices, out_ref, a):
    channels = out_ref.shape[0] // GROUP
    rows = 9 * channels
    for j, matrix_ref in enumerate(matrices):
        product = jnp.dot(
            matrix_ref[a * rows : (a + 1) * rows],
            field_ref[...],
            preferred_element_type=jnp.float32,
        )
        block = block_rows(place_ref, "part", j, channels)
        out_ref[block, :] = folded(product, channels).astype(out_ref.dtype)


def after_kernel(place_ref, *refs):
    halves, matrices = refs[: 2 * GROUP], refs[2 * GROUP : 3 * GROUP]
    field_ref, after_ref = refs[3 * GROUP :]
    for k, part_ref in enumerate(halves):
        half = part_ref.shape[0]
        start = partner(place_ref, "run", k // 2) * 2 * half + (k % 2) * half
        field_ref[pl.ds(pl.multiple_of(start, half), half), :] = part_ref[...]
    edge_sums(place_ref, field_ref, matrices, after_ref, 0)


def before_kernel(place_ref, field_ref, *refs):
    edge_sums(place_ref, field_ref, refs[:GROUP], refs[GROUP], 2)


def centre_kernel(place_ref, field_ref, *refs):
    edge_sums(place_ref, field_ref, refs[:GROUP], refs[GROUP], 1)


def gate_kernel(place_ref, same_ref, before_ref, after_ref, *refs, last):
    cotangents, active_ref, grad_ref = refs[:GROUP], refs[GROUP], refs[GROUP + 1]
    channels = cotangents[0].shape[0]
    for j, cotangent_ref in enumerate(cotangents):
        block = block_rows(place_ref, "part", j, channels)
        pre = (
            same_ref[block, :]
            + unless(at_end(place_ref, last), before_ref[block, :].astype(jnp.float32))
            + unless(at_end(place_ref, None), after_ref[block, :].astype(jnp.float32))
        )
        sigma = jax.nn.sigmoid(pre)
        active_ref[block, :] = (pre * sigma).astype(active_ref.dtype)
        grad_ref[block, :] = (
            cotangent_ref[...].astype(jnp.float32) * sigma * (1.0 + pre * (1.0 - sigma))
        ).astype(grad_ref.dtype)


def fill_moved(place_ref, moved_ref, grad_ref, low_ref, high_ref, last):
    plane = grad_ref.shape[1]
    stride = plane + 2 * BREADTH
    gap = jnp.zeros((grad_ref.shape[0], BREADTH), moved_ref.dtype)
    for p, ref in enumerate((low_ref, grad_ref, high_ref)):
        source = ref[...].astype(jnp.float32)
        if p != 1:
            source = unless(at_end(place_ref, last if p else None), source)
        for c in range(3):
            moved_ref[c, :, p * stride : p * stride + BREADTH] = gap
            moved_ref[c, :, p * stride + BREADTH : p * stride + BREADTH + plane] = lane_shifted(
                source, 1 - c
            ).astype(moved_ref.dtype)
            moved_ref[c, :, (p + 1) * stride - BREADTH : (p + 1) * stride] = gap


def tap_rows(moved_ref, block, plane):
    stride = plane + 2 * BREADTH
    parts = []
    for a in range(3):
        for b in range(3):
            for c in range(3):
                at = (2 - a) * stride + (2 - b) * BREADTH
                parts.append(moved_ref[c, block, at : at + plane])
    return jnp.concatenate(parts, axis=0)


def filter_kernel(place_ref, field_ref, grad_ref, low_ref, high_ref, *refs, last):
    outs, moved_ref = refs[:GROUP], refs[GROUP]
    rows, plane = grad_ref.shape
    fill_moved(place_ref, moved_ref, grad_ref, low_ref, high_ref, last)
    for j, out_ref in enumerate(outs):
        sums = lax.dot_general(
            field_ref[...],
            tap_rows(moved_ref, block_rows(place_ref, "part", j, rows // GROUP), plane),
            (((1,), (1,)), ((), ())),
            preferred_element_type=jnp.float32,
        )
        out_ref[...] = sums.astype(out_ref.dtype)


def input_kernel(place_ref, grad_ref, low_ref, high_ref, *refs, last):
    matrices, outs = refs[:GROUP], refs[GROUP : GROUP + 7]
    moved_ref, sum_ref = refs[GROUP + 7 :]
    rows, plane = grad_ref.shape
    fill_moved(place_ref, moved_ref, grad_ref, low_ref, high_ref, last)
    for j, matrix_ref in enumerate(matrices):
        part = lax.dot_general(
            matrix_ref[...],
            tap_rows(moved_ref, block_rows(place_ref, "part", j, rows // GROUP), plane),
            (((0,), (0,)), ((), ())),
            preferred_element_type=jnp.float32,
        )
        if j == 0:
            sum_ref[...] = part
        else:
            sum_ref[...] += part
    half = outs[1].shape[0]
    for out_ref, (j, start) in zip(outs, INPUT_CUTS):
        start = partner(place_ref, "run", j) * 2 * half + start * half
        block = pl.ds(pl.multiple_of(start, half), out_ref.shape[0])
        out_ref[...] = sum_ref[block, :].astype(out_ref.dtype)


INPUT_CUTS = ((0, 0), (2, 0), (2, 1), (1, 0), (3, 1), (1, 1), (3, 0))


def join_kernel(place_ref, near_ref, other_ref, high_ref, low_ref, near_out, other_out):
    del place_ref
    near_out[...] = (near_ref[...] + high_ref[...].astype(jnp.float32)).astype(near_out.dtype)
    other_out[...] = (other_ref[...] + low_ref[...].astype(jnp.float32)).astype(other_out.dtype)


def lift_kernel(place_ref, value_ref, other_ref, out_ref):
    del place_ref
    total = value_ref[...].astype(jnp.float32) + other_ref[...].astype(jnp.float32)
    out_ref[...] = total.astype(out_ref.dtype)


def merge_kernel(place_ref, *refs):
    del place_ref
    values, out_ref = refs[:-1], refs[-1]
    total = values[0][...].astype(jnp.float32)
    for ref in values[1:]:
        total += ref[...].astype(jnp.float32)
    out_ref[...] = total.astype(out_ref.dtype)


def pair_kernel(place_ref, own_ref, *refs):
    halves, active_ref, outs, sum_ref = refs[:4], refs[4], refs[5 : 5 + GROUP], refs[5 + GROUP]
    half = halves[0].shape[0]
    for k in range(2):
        rows = slice(k * half, (k + 1) * half)
        sum_ref[rows, :] = (
            own_ref[rows, :]
            + halves[k][...].astype(jnp.float32)
            + halves[2 + k][...].astype(jnp.float32)
        )
    for j, out_ref in enumerate(outs):
        block = block_rows(place_ref, "part", j, out_ref.shape[1])
        out_ref[0] = active_ref[block, :]
        out_ref[1] = sum_ref[block, :].astype(out_ref.dtype)


def close_kernel(place_ref, *refs):
    pairs, outs = refs[:GROUP], refs[GROUP:]
    for j, pair_ref in enumerate(pairs):
        for k, out_ref in enumerate(outs):
            channels, _, height, breadth = out_ref.shape
            value = pair_ref[k].astype(jnp.float32).reshape(channels, height, breadth)
            out_ref[:, partner_plane(place_ref, j)] = value.astype(out_ref.dtype)


def total_kernel(place_ref, parts_ref, out_ref, *, scale):
    del place_ref
    total = parts_ref[0].astype(jnp.float32)
    for s in range(1, parts_ref.shape[0]):
        total += parts_ref[s].astype(jnp.float32)
    out_ref[...] = jnp.transpose(total * scale)


DEPTH = ("space", "part")
CHANNELS = ("run", "part")


def shifted(value, by):
    count = lax.axis_size(DEPTH)
    at = {
        space * GROUP + plane_of(space, part): space * GROUP + part
        for space in range(count // GROUP)
        for part in range(GROUP)
    }
    return lax.ppermute(value, DEPTH, [(at[i], at[(i + by) % count]) for i in range(count)])


def swap(value, axis, j):
    return lax.ppermute(value, axis, [(i, i ^ j) for i in range(lax.axis_size(axis))])


def swapped(values, axis):
    return [values[0]] + [swap(values[j], axis, j) for j in range(1, GROUP)]


def body(volume, weight, cotangent):
    batch, in_local, planes, height, breadth = volume.shape
    out_local, in_total = weight.shape[3:]
    spaces = lax.axis_size("space")
    plane = height * breadth
    rows, depth, taps = GROUP * out_local, GROUP * in_local, 27 * out_local
    half = depth // 2
    grad_scale = 1.0 / math.sqrt(batch * planes * plane * spaces)
    bf16, f32 = jnp.bfloat16, jnp.float32
    place = lax.axis_index(("space", "run", "part")).reshape(1)
    ends = {"last": spaces - 1}

    volumes = call(
        planes_kernel, [((in_local, plane), bf16)] * GROUP, "volume_planes", place, volume[0]
    )
    matrix, *cotangents = call(
        rest_kernel,
        [((taps, in_total), bf16)] + [((out_local, plane), bf16)] * GROUP,
        "rest",
        place,
        cotangent[0],
        weight.reshape(taps, in_total),
        unread=[volumes[0]],
    )
    volumes, cotangents = swapped(volumes, "part"), swapped(cotangents, "part")
    low, high = call(
        halves_kernel,
        [((half, plane), bf16)] * 2,
        "halves",
        place,
        *volumes,
        unread=[matrix],
        scratch=[pltpu.VMEM((depth, plane), bf16)],
    )
    low_1, high_3 = swap(low, "run", 1), swap(high, "run", 3)
    high_1, low_3 = swap(high, "run", 1), swap(low, "run", 3)
    low_2, high_2 = swap(low_1, "run", 3), swap(high_3, "run", 1)
    matrices = swapped([matrix] * GROUP, "part")

    field, after = call(
        after_kernel,
        [((in_total, plane), bf16), ((rows, plane), bf16)],
        "after",
        place,
        *(low, high, low_1, high_1, low_2, high_2, low_3, high_3),
        *matrices,
    )
    after = shifted(after, 1)
    (before,) = call(
        before_kernel,
        [((rows, plane), bf16)],
        "before",
        place,
        field,
        *matrices,
        unread=cotangents[1:],
    )
    (same,) = call(
        centre_kernel,
        [((rows, plane), f32)],
        "centre",
        place,
        field,
        *matrices,
        unread=[before],
    )
    before = shifted(before, -1)
    active, grad = call(
        functools.partial(gate_kernel, **ends),
        [((rows, plane), bf16)] * 2,
        "gate",
        place,
        same,
        before,
        after,
        *cotangents,
    )

    around = (grad, shifted(grad, 1), shifted(grad, -1))
    moved = pltpu.VMEM((3, rows, 3 * (plane + 2 * BREADTH)), bf16)
    sums, sums_1, sums_2, sums_3 = call(
        functools.partial(filter_kernel, **ends),
        [((in_total, taps), bf16)] * GROUP,
        "filter_sums",
        place,
        field,
        *around,
        scratch=[moved],
    )
    sums_3, sums_1 = swap(sums_3, "part", 1), swap(sums_1, "part", 1)
    own, far_low, far_high, low_1, high_3, high_1, low_3 = call(
        functools.partial(input_kernel, **ends),
        [((depth, plane), f32)] + [((half, plane), bf16)] * 4 + [((half, plane), f32)] * 2,
        "input_sums",
        place,
        *around,
        *matrices,
        unread=[sums],
        scratch=[moved, pltpu.VMEM((in_total, plane), f32)],
    )
    far_low, far_high = swap(far_low, "run", 1), swap(far_high, "run", 3)
    low_1, high_3 = swap(low_1, "run", 1), swap(high_3, "run", 3)
    (sums_2,) = call(
        lift_kernel, [((in_total, taps), bf16)], "lift", place, sums_2, sums_3, unread=[own, sums_1]
    )
    high_1, low_3 = call(
        join_kernel,
        [((half, plane), bf16)] * 2,
        "join",
        place,
        high_1,
        low_3,
        far_high,
        far_low,
        unread=[sums_2],
    )
    high_1, low_3 = swap(high_1, "run", 1), swap(low_3, "run", 3)
    sums_2 = swap(sums_2, "part", 2)
    (sums,) = call(
        merge_kernel,
        [((in_total, taps), bf16)],
        "merge",
        place,
        *(sums, sums_1, sums_2),
        unread=[low_1, high_1, low_3, high_3],
    )
    sums = lax.all_to_all(
        sums.reshape(spaces, in_total // spaces, taps),
        "space",
        split_axis=0,
        concat_axis=0,
        tiled=True,
    )
    pairs = call(
        pair_kernel,
        [((2, in_local, plane), bf16)] * GROUP,
        "pairs",
        place,
        *(own, low_1, high_1, low_3, high_3),
        active,
        scratch=[pltpu.VMEM((depth, plane), f32)],
    )
    pairs = swapped(pairs, "part")
    (total,) = call(
        functools.partial(total_kernel, scale=grad_scale),
        [((taps, in_total // spaces), f32)],
        "total",
        place,
        sums,
    )
    active, back = call(
        close_kernel,
        [((in_local, planes, height, breadth), bf16)] * 2,
        "close",
        place,
        *pairs,
    )
    return (
        active[None],
        back[None],
        total.reshape(3, 3, 3, out_local, in_total // spaces),
    )


def solution(mesh):
    spaces, filts = mesh.devices.shape
    cut = Mesh(mesh.devices.reshape(spaces, filts // GROUP, GROUP), ("space", "run", "part"))
    in_specs = (
        P(None, CHANNELS, "space", None, None),
        P(None, None, None, CHANNELS, None),
        P(None, CHANNELS, "space", None, None),
    )
    out_specs = (
        P(None, CHANNELS, "space", None, None),
        P(None, CHANNELS, "space", None, None),
        P(None, None, None, CHANNELS, "space"),
    )
    return jax.shard_map(body, mesh=cut, in_specs=in_specs, out_specs=out_specs, check_vma=False)
```

```python
import functools
import math

import jax
import jax.numpy as jnp
from jax import lax
from jax.experimental import pallas as pl
from jax.experimental.pallas import tpu as pltpu
from jax.sharding import Mesh, PartitionSpec as P

BREADTH = 128
GROUP = 4
LAYERS = 8
VMEM_LIMIT = 40 * 1024 * 1024


def lane_shifted(value, by):
    if by == 0:
        return value
    lanes = value.shape[1]
    column = lax.broadcasted_iota(jnp.int32, value.shape, 1) % BREADTH
    moved = pltpu.roll(value, (-by) % lanes, 1)
    return jnp.where(column == (BREADTH - 1 if by > 0 else 0), 0.0, moved)


def row_shifted(value, by):
    if by == 0:
        return value
    gap = jnp.zeros((value.shape[0], BREADTH), value.dtype)
    if by > 0:
        return jnp.concatenate([value[:, BREADTH:], gap], axis=1)
    return jnp.concatenate([gap, value[:, :-BREADTH]], axis=1)


def folded(product, channels):
    total = None
    for c in range(3):
        column = None
        for b in range(3):
            at = (b * 3 + c) * channels
            part = row_shifted(product[at : at + channels], b - 1)
            column = part if column is None else column + part
        column = lane_shifted(column, c - 1)
        total = column if total is None else total + column
    return total


def partner(place_ref, axis, j):
    step = {"part": 1, "run": GROUP}[axis]
    return ((place_ref[0] // step) % GROUP) ^ j


def plane_of(space, part):
    backwards = (1 + space + space // LAYERS) % 2
    return part ^ (part // 2) ^ (backwards * (GROUP - 1))


def partner_plane(place_ref, j):
    return plane_of(place_ref[0] // GROUP**2, (place_ref[0] % GROUP) ^ j)


def at_end(place_ref, last):
    space, plane = place_ref[0] // GROUP**2, partner_plane(place_ref, 0)
    if last is None:
        return (space == 0) & (plane == 0)
    return (space == last) & (plane == GROUP - 1)


def unless(condition, value):
    return jnp.where(condition, jnp.zeros_like(value), value)


def block_rows(place_ref, axis, j, rows):
    return pl.ds(pl.multiple_of(partner(place_ref, axis, j) * rows, rows), rows)


def call(kernel, outputs, name, place, *operands, unread=(), scratch=(), flops=1):
    def run(place_ref, *refs):
        kernel(place_ref, *refs[: len(operands)], *refs[len(operands) + len(unread) :])

    return pl.pallas_call(
        run,
        in_specs=[pl.BlockSpec(memory_space=pltpu.SMEM)]
        + [pl.BlockSpec(memory_space=pltpu.VMEM)] * len(operands)
        + [pl.BlockSpec(memory_space=pl.ANY)] * len(unread),
        out_specs=[pl.BlockSpec(memory_space=pltpu.VMEM)] * len(outputs),
        out_shape=[jax.ShapeDtypeStruct(shape, dtype) for shape, dtype in outputs],
        scratch_shapes=list(scratch),
        compiler_params=pltpu.CompilerParams(vmem_limit_bytes=VMEM_LIMIT),
        cost_estimate=pl.CostEstimate(flops=flops, bytes_accessed=1, transcendentals=0),
        name=name,
    )(place, *operands, *unread)


def planes_kernel(place_ref, value_ref, *outs):
    channels, _, height, breadth = value_ref.shape
    for j, out_ref in enumerate(outs):
        value = value_ref[:, partner_plane(place_ref, j)].astype(jnp.float32)
        out_ref[...] = value.reshape(channels, height * breadth).astype(out_ref.dtype)


def rest_kernel(place_ref, cotangent_ref, filters_ref, matrix_ref, *outs):
    planes_kernel(place_ref, cotangent_ref, *outs)
    matrix_ref[...] = filters_ref[...]


def order_kernel(place_ref, *refs):
    pieces, (out_ref,) = refs[:GROUP], refs[GROUP:]
    for j, piece_ref in enumerate(pieces):
        out_ref[block_rows(place_ref, "part", j, piece_ref.shape[0]), :] = piece_ref[...]


def cut_kernel(place_ref, near_ref, other_ref, low_ref, high_ref):
    del place_ref
    half = low_ref.shape[0]
    low_ref[...] = near_ref[:half]
    high_ref[...] = other_ref[half:]


def edge_sums(place_ref, field_ref, matrices, out_ref, a):
    channels = out_ref.shape[0] // GROUP
    rows = 9 * channels
    for j, matrix_ref in enumerate(matrices):
        product = jnp.dot(
            matrix_ref[a * rows : (a + 1) * rows],
            field_ref[...],
            preferred_element_type=jnp.float32,
        )
        block = block_rows(place_ref, "part", j, channels)
        out_ref[block, :] = folded(product, channels).astype(out_ref.dtype)


def after_kernel(place_ref, *refs):
    blocks, halves, matrices = refs[:3], refs[3:5], refs[5 : 5 + GROUP]
    field_ref, after_ref = refs[5 + GROUP :]
    for j, ref in zip((0, 1, 3), blocks):
        field_ref[block_rows(place_ref, "run", j, ref.shape[0]), :] = ref[...]
    for k, ref in enumerate(halves):
        half = ref.shape[0]
        start = (partner(place_ref, "run", 2) * 2 + k) * half
        field_ref[pl.ds(pl.multiple_of(start, half), half), :] = ref[...]
    edge_sums(place_ref, field_ref, matrices, after_ref, 0)


def before_kernel(place_ref, field_ref, *refs):
    edge_sums(place_ref, field_ref, refs[:GROUP], refs[GROUP], 2)


def centre_kernel(place_ref, field_ref, *refs):
    edge_sums(place_ref, field_ref, refs[:GROUP], refs[GROUP], 1)


def gate_kernel(place_ref, same_ref, before_ref, after_ref, *refs, last):
    cotangents, active_ref, grad_ref = refs[:GROUP], refs[GROUP], refs[GROUP + 1]
    channels = cotangents[0].shape[0]
    for j, cotangent_ref in enumerate(cotangents):
        block = block_rows(place_ref, "part", j, channels)
        pre = (
            same_ref[block, :]
            + unless(at_end(place_ref, last), before_ref[block, :].astype(jnp.float32))
            + unless(at_end(place_ref, None), after_ref[block, :].astype(jnp.float32))
        )
        sigma = jax.nn.sigmoid(pre)
        active_ref[block, :] = (pre * sigma).astype(active_ref.dtype)
        grad_ref[block, :] = (
            cotangent_ref[...].astype(jnp.float32) * sigma * (1.0 + pre * (1.0 - sigma))
        ).astype(grad_ref.dtype)


def fill_moved(place_ref, moved_ref, grad_ref, low_ref, high_ref, last):
    plane = grad_ref.shape[1]
    stride = plane + 2 * BREADTH
    gap = jnp.zeros((grad_ref.shape[0], BREADTH), moved_ref.dtype)
    for p, ref in enumerate((low_ref, grad_ref, high_ref)):
        source = ref[...].astype(jnp.float32)
        if p != 1:
            source = unless(at_end(place_ref, last if p else None), source)
        for c in range(3):
            moved_ref[c, :, p * stride : p * stride + BREADTH] = gap
            moved_ref[c, :, p * stride + BREADTH : p * stride + BREADTH + plane] = lane_shifted(
                source, 1 - c
            ).astype(moved_ref.dtype)
            moved_ref[c, :, (p + 1) * stride - BREADTH : (p + 1) * stride] = gap


def tap_rows(moved_ref, block, plane):
    stride = plane + 2 * BREADTH
    parts = []
    for a in range(3):
        for b in range(3):
            for c in range(3):
                at = (2 - a) * stride + (2 - b) * BREADTH
                parts.append(moved_ref[c, block, at : at + plane])
    return jnp.concatenate(parts, axis=0)


def filter_kernel(place_ref, field_ref, grad_ref, low_ref, high_ref, *refs, last):
    outs, moved_ref = refs[:GROUP], refs[GROUP]
    rows, plane = grad_ref.shape
    fill_moved(place_ref, moved_ref, grad_ref, low_ref, high_ref, last)
    for j, out_ref in enumerate(outs):
        sums = lax.dot_general(
            field_ref[...],
            tap_rows(moved_ref, block_rows(place_ref, "part", j, rows // GROUP), plane),
            (((1,), (1,)), ((), ())),
            preferred_element_type=jnp.float32,
        )
        out_ref[...] = sums.astype(out_ref.dtype)


def input_kernel(place_ref, grad_ref, low_ref, high_ref, *refs, last):
    matrices, outs = refs[:GROUP], refs[GROUP : GROUP + 7]
    moved_ref, sum_ref = refs[GROUP + 7 :]
    rows, plane = grad_ref.shape
    fill_moved(place_ref, moved_ref, grad_ref, low_ref, high_ref, last)
    for j, matrix_ref in enumerate(matrices):
        part = lax.dot_general(
            matrix_ref[...],
            tap_rows(moved_ref, block_rows(place_ref, "part", j, rows // GROUP), plane),
            (((0,), (0,)), ((), ())),
            preferred_element_type=jnp.float32,
        )
        if j == 0:
            sum_ref[...] = part
        else:
            sum_ref[...] += part
    half = outs[1].shape[0]
    for out_ref, (j, start) in zip(outs, INPUT_CUTS):
        start = partner(place_ref, "run", j) * 2 * half + start * half
        block = pl.ds(pl.multiple_of(start, half), out_ref.shape[0])
        out_ref[...] = sum_ref[block, :].astype(out_ref.dtype)


INPUT_CUTS = ((0, 0), (2, 0), (2, 1), (1, 0), (3, 1), (1, 1), (3, 0))


def join_kernel(place_ref, near_ref, other_ref, high_ref, low_ref, near_out, other_out):
    del place_ref
    near_out[...] = (near_ref[...] + high_ref[...].astype(jnp.float32)).astype(near_out.dtype)
    other_out[...] = (other_ref[...] + low_ref[...].astype(jnp.float32)).astype(other_out.dtype)


def lift_kernel(place_ref, value_ref, other_ref, out_ref):
    del place_ref
    total = value_ref[...].astype(jnp.float32) + other_ref[...].astype(jnp.float32)
    out_ref[...] = total.astype(out_ref.dtype)


def merge_kernel(place_ref, *refs):
    del place_ref
    values, out_ref = refs[:-1], refs[-1]
    total = values[0][...].astype(jnp.float32)
    for ref in values[1:]:
        total += ref[...].astype(jnp.float32)
    out_ref[...] = total.astype(out_ref.dtype)


def pair_kernel(place_ref, own_ref, *refs):
    halves, active_ref, outs, sum_ref = refs[:4], refs[4], refs[5 : 5 + GROUP], refs[5 + GROUP]
    half = halves[0].shape[0]
    for k in range(2):
        rows = slice(k * half, (k + 1) * half)
        sum_ref[rows, :] = (
            own_ref[rows, :]
            + halves[k][...].astype(jnp.float32)
            + halves[2 + k][...].astype(jnp.float32)
        )
    for j, out_ref in enumerate(outs):
        block = block_rows(place_ref, "part", j, out_ref.shape[1])
        out_ref[0] = active_ref[block, :]
        out_ref[1] = sum_ref[block, :].astype(out_ref.dtype)


def close_kernel(place_ref, *refs):
    pairs, outs = refs[:GROUP], refs[GROUP:]
    for j, pair_ref in enumerate(pairs):
        for k, out_ref in enumerate(outs):
            channels, _, height, breadth = out_ref.shape
            value = pair_ref[k].astype(jnp.float32).reshape(channels, height, breadth)
            out_ref[:, partner_plane(place_ref, j)] = value.astype(out_ref.dtype)


def total_kernel(place_ref, parts_ref, out_ref, *, scale):
    del place_ref
    total = parts_ref[0].astype(jnp.float32)
    for s in range(1, parts_ref.shape[0]):
        total += parts_ref[s].astype(jnp.float32)
    out_ref[...] = jnp.transpose(total * scale)


DEPTH = ("space", "part")
CHANNELS = ("run", "part")


def shifted(value, by):
    count = lax.axis_size(DEPTH)
    at = {
        space * GROUP + plane_of(space, part): space * GROUP + part
        for space in range(count // GROUP)
        for part in range(GROUP)
    }
    return lax.ppermute(value, DEPTH, [(at[i], at[(i + by) % count]) for i in range(count)])


def swap(value, axis, j):
    return lax.ppermute(value, axis, [(i, i ^ j) for i in range(lax.axis_size(axis))])


def swapped(values, axis):
    return [values[0]] + [swap(values[j], axis, j) for j in range(1, GROUP)]


def body(volume, weight, cotangent):
    batch, in_local, planes, height, breadth = volume.shape
    out_local, in_total = weight.shape[3:]
    spaces = lax.axis_size("space")
    plane = height * breadth
    rows, depth, taps = GROUP * out_local, GROUP * in_local, 27 * out_local
    half = depth // 2
    grad_scale = 1.0 / math.sqrt(batch * planes * plane * spaces)
    bf16, f32 = jnp.bfloat16, jnp.float32
    place = lax.axis_index(("space", "run", "part")).reshape(1)
    ends = {"last": spaces - 1}

    volumes = call(
        planes_kernel, [((in_local, plane), bf16)] * GROUP, "volume_planes", place, volume[0]
    )
    matrix, *cotangents = call(
        rest_kernel,
        [((taps, in_total), bf16)] + [((out_local, plane), bf16)] * GROUP,
        "rest",
        place,
        cotangent[0],
        weight.reshape(taps, in_total),
        unread=[volumes[0]],
    )
    volumes, cotangents = swapped(volumes, "part"), swapped(cotangents, "part")
    (block,) = call(
        order_kernel, [((depth, plane), bf16)], "order", place, *volumes, unread=[matrix]
    )
    block_1, block_3 = swap(block, "run", 1), swap(block, "run", 3)
    low_2, high_2 = call(
        cut_kernel, [((half, plane), bf16)] * 2, "cut", place, block_1, block_3
    )
    low_2, high_2 = swap(low_2, "run", 3), swap(high_2, "run", 1)
    matrices = swapped([matrix] * GROUP, "part")

    field, after = call(
        after_kernel,
        [((in_total, plane), bf16), ((rows, plane), bf16)],
        "after",
        place,
        *(block, block_1, block_3, low_2, high_2),
        *matrices,
    )
    after = shifted(after, 1)
    (before,) = call(
        before_kernel,
        [((rows, plane), bf16)],
        "before",
        place,
        field,
        *matrices,
        unread=cotangents[1:],
    )
    (same,) = call(
        centre_kernel,
        [((rows, plane), f32)],
        "centre",
        place,
        field,
        *matrices,
        unread=[before],
    )
    before = shifted(before, -1)
    active, grad = call(
        functools.partial(gate_kernel, **ends),
        [((rows, plane), bf16)] * 2,
        "gate",
        place,
        same,
        before,
        after,
        *cotangents,
    )

    around = (grad, shifted(grad, 1), shifted(grad, -1))
    moved = pltpu.VMEM((3, rows, 3 * (plane + 2 * BREADTH)), bf16)
    sums, sums_1, sums_2, sums_3 = call(
        functools.partial(filter_kernel, **ends),
        [((in_total, taps), bf16)] * GROUP,
        "filter_sums",
        place,
        field,
        *around,
        scratch=[moved],
    )
    sums_3, sums_1 = swap(sums_3, "part", 1), swap(sums_1, "part", 1)
    own, far_low, far_high, low_1, high_3, high_1, low_3 = call(
        functools.partial(input_kernel, **ends),
        [((depth, plane), f32)] + [((half, plane), bf16)] * 4 + [((half, plane), f32)] * 2,
        "input_sums",
        place,
        *around,
        *matrices,
        unread=[sums],
        scratch=[moved, pltpu.VMEM((in_total, plane), f32)],
    )
    far_low, far_high = swap(far_low, "run", 1), swap(far_high, "run", 3)
    low_1, high_3 = swap(low_1, "run", 1), swap(high_3, "run", 3)
    (sums_2,) = call(
        lift_kernel, [((in_total, taps), bf16)], "lift", place, sums_2, sums_3, unread=[own, sums_1]
    )
    high_1, low_3 = call(
        join_kernel,
        [((half, plane), bf16)] * 2,
        "join",
        place,
        high_1,
        low_3,
        far_high,
        far_low,
        unread=[sums_2],
    )
    high_1, low_3 = swap(high_1, "run", 1), swap(low_3, "run", 3)
    sums_2 = swap(sums_2, "part", 2)
    (sums,) = call(
        merge_kernel,
        [((in_total, taps), bf16)],
        "merge",
        place,
        *(sums, sums_1, sums_2),
        unread=[low_1, high_3],
    )
    sums = lax.all_to_all(
        sums.reshape(spaces, in_total // spaces, taps),
        "space",
        split_axis=0,
        concat_axis=0,
        tiled=True,
    )
    pairs = call(
        pair_kernel,
        [((2, in_local, plane), bf16)] * GROUP,
        "pairs",
        place,
        *(own, low_1, high_1, low_3, high_3),
        active,
        scratch=[pltpu.VMEM((depth, plane), f32)],
    )
    pairs = swapped(pairs, "part")
    (total,) = call(
        functools.partial(total_kernel, scale=grad_scale),
        [((taps, in_total // spaces), f32)],
        "total",
        place,
        sums,
    )
    active, back = call(
        close_kernel,
        [((in_local, planes, height, breadth), bf16)] * 2,
        "close",
        place,
        *pairs,
    )
    return (
        active[None],
        back[None],
        total.reshape(3, 3, 3, out_local, in_total // spaces),
    )


def solution(mesh):
    spaces, filts = mesh.devices.shape
    cut = Mesh(mesh.devices.reshape(spaces, filts // GROUP, GROUP), ("space", "run", "part"))
    in_specs = (
        P(None, CHANNELS, "space", None, None),
        P(None, None, None, CHANNELS, None),
        P(None, CHANNELS, "space", None, None),
    )
    out_specs = (
        P(None, CHANNELS, "space", None, None),
        P(None, CHANNELS, "space", None, None),
        P(None, None, None, CHANNELS, "space"),
    )
    return jax.shard_map(body, mesh=cut, in_specs=in_specs, out_specs=out_specs, check_vma=False)
```

```python
import functools
import math

import jax
import jax.numpy as jnp
from jax import lax
from jax.experimental import pallas as pl
from jax.experimental.pallas import tpu as pltpu
from jax.sharding import Mesh, PartitionSpec as P

BREADTH = 128
GROUP = 4
LAYERS = 8
VMEM_LIMIT = 40 * 1024 * 1024


def lane_shifted(value, by):
    if by == 0:
        return value
    lanes = value.shape[1]
    column = lax.broadcasted_iota(jnp.int32, value.shape, 1) % BREADTH
    moved = pltpu.roll(value, (-by) % lanes, 1)
    return jnp.where(column == (BREADTH - 1 if by > 0 else 0), 0.0, moved)


def row_shifted(value, by):
    if by == 0:
        return value
    gap = jnp.zeros((value.shape[0], BREADTH), value.dtype)
    if by > 0:
        return jnp.concatenate([value[:, BREADTH:], gap], axis=1)
    return jnp.concatenate([gap, value[:, :-BREADTH]], axis=1)


def folded(product, channels):
    total = None
    for c in range(3):
        column = None
        for b in range(3):
            at = (b * 3 + c) * channels
            part = row_shifted(product[at : at + channels], b - 1)
            column = part if column is None else column + part
        column = lane_shifted(column, c - 1)
        total = column if total is None else total + column
    return total


def partner(place_ref, axis, j):
    step = {"part": 1, "run": GROUP}[axis]
    return ((place_ref[0] // step) % GROUP) ^ j


def plane_of(space, part):
    backwards = (1 + space + space // LAYERS) % 2
    return part ^ (part // 2) ^ (backwards * (GROUP - 1))


def partner_plane(place_ref, j):
    return plane_of(place_ref[0] // GROUP**2, (place_ref[0] % GROUP) ^ j)


def at_end(place_ref, last):
    space, plane = place_ref[0] // GROUP**2, partner_plane(place_ref, 0)
    if last is None:
        return (space == 0) & (plane == 0)
    return (space == last) & (plane == GROUP - 1)


def unless(condition, value):
    return jnp.where(condition, jnp.zeros_like(value), value)


def block_rows(place_ref, axis, j, rows):
    return pl.ds(pl.multiple_of(partner(place_ref, axis, j) * rows, rows), rows)


def call(kernel, outputs, name, place, *operands, unread=(), scratch=(), flops=1):
    def run(place_ref, *refs):
        kernel(place_ref, *refs[: len(operands)], *refs[len(operands) + len(unread) :])

    return pl.pallas_call(
        run,
        in_specs=[pl.BlockSpec(memory_space=pltpu.SMEM)]
        + [pl.BlockSpec(memory_space=pltpu.VMEM)] * len(operands)
        + [pl.BlockSpec(memory_space=pl.ANY)] * len(unread),
        out_specs=[pl.BlockSpec(memory_space=pltpu.VMEM)] * len(outputs),
        out_shape=[jax.ShapeDtypeStruct(shape, dtype) for shape, dtype in outputs],
        scratch_shapes=list(scratch),
        compiler_params=pltpu.CompilerParams(vmem_limit_bytes=VMEM_LIMIT),
        cost_estimate=pl.CostEstimate(flops=flops, bytes_accessed=1, transcendentals=0),
        name=name,
    )(place, *operands, *unread)


def planes_kernel(place_ref, value_ref, *outs):
    channels, _, height, breadth = value_ref.shape
    for j, out_ref in enumerate(outs):
        value = value_ref[:, partner_plane(place_ref, j)].astype(jnp.float32)
        out_ref[...] = value.reshape(channels, height * breadth).astype(out_ref.dtype)


def rest_kernel(place_ref, cotangent_ref, filters_ref, matrix_ref, *outs):
    planes_kernel(place_ref, cotangent_ref, *outs)
    matrix_ref[...] = filters_ref[...]


def order_kernel(place_ref, *refs):
    pieces, (out_ref,) = refs[:GROUP], refs[GROUP:]
    for j, piece_ref in enumerate(pieces):
        out_ref[block_rows(place_ref, "part", j, piece_ref.shape[0]), :] = piece_ref[...]


def cut_kernel(place_ref, near_ref, other_ref, low_ref, high_ref):
    del place_ref
    half = low_ref.shape[0]
    low_ref[...] = near_ref[:half]
    high_ref[...] = other_ref[half:]


def edge_sums(place_ref, field_ref, matrices, out_ref, a):
    channels = out_ref.shape[0] // GROUP
    rows = 9 * channels
    for j, matrix_ref in enumerate(matrices):
        product = jnp.dot(
            matrix_ref[a * rows : (a + 1) * rows],
            field_ref[...],
            preferred_element_type=jnp.float32,
        )
        block = block_rows(place_ref, "part", j, channels)
        out_ref[block, :] = folded(product, channels).astype(out_ref.dtype)


def after_kernel(place_ref, *refs):
    blocks, halves, matrices = refs[:3], refs[3:5], refs[5 : 5 + GROUP]
    field_ref, after_ref = refs[5 + GROUP :]
    for j, ref in zip((0, 1, 3), blocks):
        field_ref[block_rows(place_ref, "run", j, ref.shape[0]), :] = ref[...]
    for k, ref in enumerate(halves):
        half = ref.shape[0]
        start = (partner(place_ref, "run", 2) * 2 + k) * half
        field_ref[pl.ds(pl.multiple_of(start, half), half), :] = ref[...]
    edge_sums(place_ref, field_ref, matrices, after_ref, 0)


def before_kernel(place_ref, field_ref, *refs):
    edge_sums(place_ref, field_ref, refs[:GROUP], refs[GROUP], 2)


def centre_kernel(place_ref, field_ref, *refs):
    edge_sums(place_ref, field_ref, refs[:GROUP], refs[GROUP], 1)


def gate_kernel(place_ref, same_ref, before_ref, after_ref, *refs, last):
    cotangents, active_ref, grad_ref = refs[:GROUP], refs[GROUP], refs[GROUP + 1]
    channels = cotangents[0].shape[0]
    for j, cotangent_ref in enumerate(cotangents):
        block = block_rows(place_ref, "part", j, channels)
        pre = (
            same_ref[block, :]
            + unless(at_end(place_ref, last), before_ref[block, :].astype(jnp.float32))
            + unless(at_end(place_ref, None), after_ref[block, :].astype(jnp.float32))
        )
        sigma = jax.nn.sigmoid(pre)
        active_ref[block, :] = (pre * sigma).astype(active_ref.dtype)
        grad_ref[block, :] = (
            cotangent_ref[...].astype(jnp.float32) * sigma * (1.0 + pre * (1.0 - sigma))
        ).astype(grad_ref.dtype)


def fill_moved(place_ref, moved_ref, grad_ref, low_ref, high_ref, last):
    plane = grad_ref.shape[1]
    stride = plane + 2 * BREADTH
    gap = jnp.zeros((grad_ref.shape[0], BREADTH), moved_ref.dtype)
    for p, ref in enumerate((low_ref, grad_ref, high_ref)):
        source = ref[...].astype(jnp.float32)
        if p != 1:
            source = unless(at_end(place_ref, last if p else None), source)
        for c in range(3):
            moved_ref[c, :, p * stride : p * stride + BREADTH] = gap
            moved_ref[c, :, p * stride + BREADTH : p * stride + BREADTH + plane] = lane_shifted(
                source, 1 - c
            ).astype(moved_ref.dtype)
            moved_ref[c, :, (p + 1) * stride - BREADTH : (p + 1) * stride] = gap


def tap_rows(moved_ref, block, plane):
    stride = plane + 2 * BREADTH
    parts = []
    for a in range(3):
        for b in range(3):
            for c in range(3):
                at = (2 - a) * stride + (2 - b) * BREADTH
                parts.append(moved_ref[c, block, at : at + plane])
    return jnp.concatenate(parts, axis=0)


def filter_kernel(place_ref, field_ref, grad_ref, low_ref, high_ref, *refs, last):
    outs, moved_ref = refs[:GROUP], refs[GROUP]
    rows, plane = grad_ref.shape
    fill_moved(place_ref, moved_ref, grad_ref, low_ref, high_ref, last)
    for j, out_ref in enumerate(outs):
        sums = lax.dot_general(
            field_ref[...],
            tap_rows(moved_ref, block_rows(place_ref, "part", j, rows // GROUP), plane),
            (((1,), (1,)), ((), ())),
            preferred_element_type=jnp.float32,
        )
        out_ref[...] = sums.astype(out_ref.dtype)


def input_kernel(place_ref, grad_ref, low_ref, high_ref, *refs, last):
    matrices, outs = refs[:GROUP], refs[GROUP : GROUP + 7]
    moved_ref, sum_ref = refs[GROUP + 7 :]
    rows, plane = grad_ref.shape
    fill_moved(place_ref, moved_ref, grad_ref, low_ref, high_ref, last)
    for j, matrix_ref in enumerate(matrices):
        part = lax.dot_general(
            matrix_ref[...],
            tap_rows(moved_ref, block_rows(place_ref, "part", j, rows // GROUP), plane),
            (((0,), (0,)), ((), ())),
            preferred_element_type=jnp.float32,
        )
        if j == 0:
            sum_ref[...] = part
        else:
            sum_ref[...] += part
    half = outs[1].shape[0]
    for out_ref, (j, start) in zip(outs, INPUT_CUTS):
        start = partner(place_ref, "run", j) * 2 * half + start * half
        block = pl.ds(pl.multiple_of(start, half), out_ref.shape[0])
        out_ref[...] = sum_ref[block, :].astype(out_ref.dtype)


INPUT_CUTS = ((0, 0), (2, 0), (2, 1), (1, 0), (3, 1), (1, 1), (3, 0))


def join_kernel(place_ref, near_ref, other_ref, high_ref, low_ref, near_out, other_out):
    del place_ref
    near_out[...] = (near_ref[...] + high_ref[...].astype(jnp.float32)).astype(near_out.dtype)
    other_out[...] = (other_ref[...] + low_ref[...].astype(jnp.float32)).astype(other_out.dtype)


def lift_kernel(place_ref, value_ref, other_ref, out_ref):
    del place_ref
    total = value_ref[...].astype(jnp.float32) + other_ref[...].astype(jnp.float32)
    out_ref[...] = total.astype(out_ref.dtype)


def merge_kernel(place_ref, *refs):
    del place_ref
    values, out_ref = refs[:-1], refs[-1]
    total = values[0][...].astype(jnp.float32)
    for ref in values[1:]:
        total += ref[...].astype(jnp.float32)
    out_ref[...] = total.astype(out_ref.dtype)


def pair_kernel(place_ref, own_ref, *refs):
    halves, active_ref, outs, sum_ref = refs[:4], refs[4], refs[5 : 5 + GROUP], refs[5 + GROUP]
    half = halves[0].shape[0]
    for k in range(2):
        rows = slice(k * half, (k + 1) * half)
        sum_ref[rows, :] = (
            own_ref[rows, :]
            + halves[k][...].astype(jnp.float32)
            + halves[2 + k][...].astype(jnp.float32)
        )
    for j, out_ref in enumerate(outs):
        block = block_rows(place_ref, "part", j, out_ref.shape[1])
        out_ref[0] = active_ref[block, :]
        out_ref[1] = sum_ref[block, :].astype(out_ref.dtype)


def close_kernel(place_ref, *refs):
    pairs, outs = refs[:GROUP], refs[GROUP:]
    for j, pair_ref in enumerate(pairs):
        for k, out_ref in enumerate(outs):
            channels, _, height, breadth = out_ref.shape
            value = pair_ref[k].astype(jnp.float32).reshape(channels, height, breadth)
            out_ref[:, partner_plane(place_ref, j)] = value.astype(out_ref.dtype)


def total_kernel(place_ref, parts_ref, out_ref, *, scale):
    del place_ref
    total = parts_ref[0].astype(jnp.float32)
    for s in range(1, parts_ref.shape[0]):
        total += parts_ref[s].astype(jnp.float32)
    out_ref[...] = jnp.transpose(total * scale)


DEPTH = ("space", "part")
CHANNELS = ("run", "part")


def shifted(value, by):
    count = lax.axis_size(DEPTH)
    at = {
        space * GROUP + plane_of(space, part): space * GROUP + part
        for space in range(count // GROUP)
        for part in range(GROUP)
    }
    return lax.ppermute(value, DEPTH, [(at[i], at[(i + by) % count]) for i in range(count)])


def swap(value, axis, j):
    return lax.ppermute(value, axis, [(i, i ^ j) for i in range(lax.axis_size(axis))])


def swapped(values, axis):
    return [values[0]] + [swap(values[j], axis, j) for j in range(1, GROUP)]


def body(volume, weight, cotangent):
    batch, in_local, planes, height, breadth = volume.shape
    out_local, in_total = weight.shape[3:]
    spaces = lax.axis_size("space")
    plane = height * breadth
    rows, depth, taps = GROUP * out_local, GROUP * in_local, 27 * out_local
    half = depth // 2
    grad_scale = 1.0 / math.sqrt(batch * planes * plane * spaces)
    bf16, f32 = jnp.bfloat16, jnp.float32
    place = lax.axis_index(("space", "run", "part")).reshape(1)
    ends = {"last": spaces - 1}

    volumes = call(
        planes_kernel, [((in_local, plane), bf16)] * GROUP, "volume_planes", place, volume[0]
    )
    matrix, *cotangents = call(
        rest_kernel,
        [((taps, in_total), bf16)] + [((out_local, plane), bf16)] * GROUP,
        "rest",
        place,
        cotangent[0],
        weight.reshape(taps, in_total),
        unread=[volumes[0]],
    )
    volumes, cotangents = swapped(volumes, "part"), swapped(cotangents, "part")
    (block,) = call(
        order_kernel, [((depth, plane), bf16)], "order", place, *volumes, unread=[matrix]
    )
    block_1, block_3 = swap(block, "run", 1), swap(block, "run", 3)
    low_2, high_2 = call(
        cut_kernel, [((half, plane), bf16)] * 2, "cut", place, block_1, block_3
    )
    low_2, high_2 = swap(low_2, "run", 3), swap(high_2, "run", 1)
    matrices = swapped([matrix] * GROUP, "part")

    field, after = call(
        after_kernel,
        [((in_total, plane), bf16), ((rows, plane), bf16)],
        "after",
        place,
        *(block, block_1, block_3, low_2, high_2),
        *matrices,
    )
    after = shifted(after, 1)
    (before,) = call(
        before_kernel,
        [((rows, plane), bf16)],
        "before",
        place,
        field,
        *matrices,
        unread=cotangents[1:],
    )
    (same,) = call(
        centre_kernel,
        [((rows, plane), f32)],
        "centre",
        place,
        field,
        *matrices,
        unread=[before],
    )
    before = shifted(before, -1)
    active, grad = call(
        functools.partial(gate_kernel, **ends),
        [((rows, plane), bf16)] * 2,
        "gate",
        place,
        same,
        before,
        after,
        *cotangents,
    )

    around = (grad, shifted(grad, 1), shifted(grad, -1))
    moved = pltpu.VMEM((3, rows, 3 * (plane + 2 * BREADTH)), bf16)
    sums, sums_1, sums_2, sums_3 = call(
        functools.partial(filter_kernel, **ends),
        [((in_total, taps), bf16)] * GROUP,
        "filter_sums",
        place,
        field,
        *around,
        scratch=[moved],
    )
    sums_3, sums_1 = swap(sums_3, "part", 1), swap(sums_1, "part", 1)
    own, far_low, far_high, low_1, high_3, high_1, low_3 = call(
        functools.partial(input_kernel, **ends),
        [((depth, plane), f32)] + [((half, plane), bf16)] * 4 + [((half, plane), f32)] * 2,
        "input_sums",
        place,
        *around,
        *matrices,
        unread=[sums],
        scratch=[moved, pltpu.VMEM((in_total, plane), f32)],
    )
    far_low, far_high = swap(far_low, "run", 1), swap(far_high, "run", 3)
    low_1, high_3 = swap(low_1, "run", 1), swap(high_3, "run", 3)
    (sums_2,) = call(
        lift_kernel, [((in_total, taps), bf16)], "lift", place, sums_2, sums_3, unread=[own, sums_1]
    )
    high_1, low_3 = call(
        join_kernel,
        [((half, plane), bf16)] * 2,
        "join",
        place,
        high_1,
        low_3,
        far_high,
        far_low,
        unread=[sums_2],
    )
    high_1, low_3 = swap(high_1, "run", 1), swap(low_3, "run", 3)
    sums_2 = swap(sums_2, "part", 2)
    (sums,) = call(
        merge_kernel,
        [((in_total, taps), bf16)],
        "merge",
        place,
        *(sums, sums_1, sums_2),
        unread=[low_1, high_1, low_3, high_3],
    )
    sums = lax.all_to_all(
        sums.reshape(spaces, in_total // spaces, taps),
        "space",
        split_axis=0,
        concat_axis=0,
        tiled=True,
    )
    pairs = call(
        pair_kernel,
        [((2, in_local, plane), bf16)] * GROUP,
        "pairs",
        place,
        *(own, low_1, high_1, low_3, high_3),
        active,
        scratch=[pltpu.VMEM((depth, plane), f32)],
    )
    pairs = swapped(pairs, "part")
    (total,) = call(
        functools.partial(total_kernel, scale=grad_scale),
        [((taps, in_total // spaces), f32)],
        "total",
        place,
        sums,
    )
    active, back = call(
        close_kernel,
        [((in_local, planes, height, breadth), bf16)] * 2,
        "close",
        place,
        *pairs,
    )
    return (
        active[None],
        back[None],
        total.reshape(3, 3, 3, out_local, in_total // spaces),
    )


def solution(mesh):
    spaces, filts = mesh.devices.shape
    cut = Mesh(mesh.devices.reshape(spaces, filts // GROUP, GROUP), ("space", "run", "part"))
    in_specs = (
        P(None, CHANNELS, "space", None, None),
        P(None, None, None, CHANNELS, None),
        P(None, CHANNELS, "space", None, None),
    )
    out_specs = (
        P(None, CHANNELS, "space", None, None),
        P(None, CHANNELS, "space", None, None),
        P(None, None, None, CHANNELS, "space"),
    )
    return jax.shard_map(body, mesh=cut, in_specs=in_specs, out_specs=out_specs, check_vma=False)
```

```python
import functools
import math

import jax
import jax.numpy as jnp
from jax import lax
from jax.experimental import pallas as pl
from jax.experimental.pallas import tpu as pltpu
from jax.sharding import Mesh, PartitionSpec as P

BREADTH = 128
GROUP = 4
LAYERS = 8
VMEM_LIMIT = 40 * 1024 * 1024


def lane_shifted(value, by):
    if by == 0:
        return value
    lanes = value.shape[1]
    column = lax.broadcasted_iota(jnp.int32, value.shape, 1) % BREADTH
    moved = pltpu.roll(value, (-by) % lanes, 1)
    return jnp.where(column == (BREADTH - 1 if by > 0 else 0), 0.0, moved)


def row_shifted(value, by):
    if by == 0:
        return value
    gap = jnp.zeros((value.shape[0], BREADTH), value.dtype)
    if by > 0:
        return jnp.concatenate([value[:, BREADTH:], gap], axis=1)
    return jnp.concatenate([gap, value[:, :-BREADTH]], axis=1)


def folded(product, channels):
    total = None
    for c in range(3):
        column = None
        for b in range(3):
            at = (b * 3 + c) * channels
            part = row_shifted(product[at : at + channels], b - 1)
            column = part if column is None else column + part
        column = lane_shifted(column, c - 1)
        total = column if total is None else total + column
    return total


def partner(place_ref, axis, j):
    step = {"part": 1, "run": GROUP}[axis]
    return ((place_ref[0] // step) % GROUP) ^ j


def plane_of(space, part):
    backwards = (1 + space + space // LAYERS) % 2
    return part ^ (part // 2) ^ (backwards * (GROUP - 1))


def partner_plane(place_ref, j):
    return plane_of(place_ref[0] // GROUP**2, (place_ref[0] % GROUP) ^ j)


def at_end(place_ref, last):
    space, plane = place_ref[0] // GROUP**2, partner_plane(place_ref, 0)
    if last is None:
        return (space == 0) & (plane == 0)
    return (space == last) & (plane == GROUP - 1)


def unless(condition, value):
    return jnp.where(condition, jnp.zeros_like(value), value)


def block_rows(place_ref, axis, j, rows):
    return pl.ds(pl.multiple_of(partner(place_ref, axis, j) * rows, rows), rows)


def call(kernel, outputs, name, place, *operands, unread=(), scratch=(), flops=1):
    def run(place_ref, *refs):
        kernel(place_ref, *refs[: len(operands)], *refs[len(operands) + len(unread) :])

    return pl.pallas_call(
        run,
        in_specs=[pl.BlockSpec(memory_space=pltpu.SMEM)]
        + [pl.BlockSpec(memory_space=pltpu.VMEM)] * len(operands)
        + [pl.BlockSpec(memory_space=pl.ANY)] * len(unread),
        out_specs=[pl.BlockSpec(memory_space=pltpu.VMEM)] * len(outputs),
        out_shape=[jax.ShapeDtypeStruct(shape, dtype) for shape, dtype in outputs],
        scratch_shapes=list(scratch),
        compiler_params=pltpu.CompilerParams(vmem_limit_bytes=VMEM_LIMIT),
        cost_estimate=pl.CostEstimate(flops=flops, bytes_accessed=1, transcendentals=0),
        name=name,
    )(place, *operands, *unread)


def planes_kernel(place_ref, value_ref, *outs):
    channels, _, height, breadth = value_ref.shape
    for j, out_ref in enumerate(outs):
        value = value_ref[:, partner_plane(place_ref, j)].astype(jnp.float32)
        out_ref[...] = value.reshape(channels, height * breadth).astype(out_ref.dtype)


def rest_kernel(place_ref, cotangent_ref, filters_ref, matrix_ref, *outs):
    planes_kernel(place_ref, cotangent_ref, *outs)
    matrix_ref[...] = filters_ref[...]


def order_kernel(place_ref, *refs):
    pieces, (out_ref,) = refs[:GROUP], refs[GROUP:]
    for j, piece_ref in enumerate(pieces):
        out_ref[block_rows(place_ref, "part", j, piece_ref.shape[0]), :] = piece_ref[...]


def cut_kernel(place_ref, near_ref, other_ref, low_ref, high_ref):
    del place_ref
    half = low_ref.shape[0]
    low_ref[...] = near_ref[:half]
    high_ref[...] = other_ref[half:]


def edge_sums(place_ref, field_ref, matrices, out_ref, a):
    channels = out_ref.shape[0] // GROUP
    rows = 9 * channels
    for j, matrix_ref in enumerate(matrices):
        product = jnp.dot(
            matrix_ref[a * rows : (a + 1) * rows],
            field_ref[...],
            preferred_element_type=jnp.float32,
        )
        block = block_rows(place_ref, "part", j, channels)
        out_ref[block, :] = folded(product, channels).astype(out_ref.dtype)


def after_kernel(place_ref, *refs):
    blocks, halves, matrices = refs[:3], refs[3:5], refs[5 : 5 + GROUP]
    field_ref, after_ref = refs[5 + GROUP :]
    for j, ref in zip((0, 1, 3), blocks):
        field_ref[block_rows(place_ref, "run", j, ref.shape[0]), :] = ref[...]
    for k, ref in enumerate(halves):
        half = ref.shape[0]
        start = (partner(place_ref, "run", 2) * 2 + k) * half
        field_ref[pl.ds(pl.multiple_of(start, half), half), :] = ref[...]
    edge_sums(place_ref, field_ref, matrices, after_ref, 0)


def before_kernel(place_ref, field_ref, *refs):
    edge_sums(place_ref, field_ref, refs[:GROUP], refs[GROUP], 2)


def centre_kernel(place_ref, field_ref, *refs):
    edge_sums(place_ref, field_ref, refs[:GROUP], refs[GROUP], 1)


def gate_kernel(place_ref, same_ref, before_ref, after_ref, *refs, last):
    cotangents, active_ref, grad_ref = refs[:GROUP], refs[GROUP], refs[GROUP + 1]
    channels = cotangents[0].shape[0]
    for j, cotangent_ref in enumerate(cotangents):
        block = block_rows(place_ref, "part", j, channels)
        pre = (
            same_ref[block, :]
            + unless(at_end(place_ref, last), before_ref[block, :].astype(jnp.float32))
            + unless(at_end(place_ref, None), after_ref[block, :].astype(jnp.float32))
        )
        sigma = jax.nn.sigmoid(pre)
        active_ref[block, :] = (pre * sigma).astype(active_ref.dtype)
        grad_ref[block, :] = (
            cotangent_ref[...].astype(jnp.float32) * sigma * (1.0 + pre * (1.0 - sigma))
        ).astype(grad_ref.dtype)


def fill_plane(moved_ref, p, source):
    rows, plane = source.shape
    start = p * (plane + 2 * BREADTH)
    gap = jnp.zeros((rows, BREADTH), moved_ref.dtype)
    source = source.astype(jnp.float32)
    for c in range(3):
        moved_ref[c, :, start : start + BREADTH] = gap
        moved_ref[c, :, start + BREADTH : start + BREADTH + plane] = lane_shifted(
            source, 1 - c
        ).astype(moved_ref.dtype)
        moved_ref[c, :, start + BREADTH + plane : start + 2 * BREADTH + plane] = gap


def fill_sides(place_ref, moved_ref, slots, low_ref, high_ref, last):
    fill_plane(moved_ref, slots[0], unless(at_end(place_ref, None), low_ref[...]))
    fill_plane(moved_ref, slots[1], unless(at_end(place_ref, last), high_ref[...]))


def tap_rows(moved_ref, block, plane, slots):
    parts = []
    for p in slots:
        for b in range(3):
            for c in range(3):
                at = p * (plane + 2 * BREADTH) + (2 - b) * BREADTH
                parts.append(moved_ref[c, block, at : at + plane])
    return jnp.concatenate(parts, axis=0)


def filter_kernel(place_ref, field_ref, grad_ref, low_ref, high_ref, *refs, last):
    outs, moved_ref = refs[:GROUP], refs[GROUP]
    rows, plane = grad_ref.shape
    fill_plane(moved_ref, 1, grad_ref[...])
    fill_sides(place_ref, moved_ref, (0, 2), low_ref, high_ref, last)
    for j, out_ref in enumerate(outs):
        block = block_rows(place_ref, "part", j, rows // GROUP)
        sums = lax.dot_general(
            field_ref[...],
            tap_rows(moved_ref, block, plane, (2, 1, 0)),
            (((1,), (1,)), ((), ())),
            preferred_element_type=jnp.float32,
        )
        out_ref[...] = sums.astype(out_ref.dtype)


def add_taps(place_ref, sum_ref, moved_ref, matrices, slots, pick, start=None):
    plane = sum_ref.shape[1]
    for j, matrix_ref in enumerate(matrices):
        taps = pick(matrix_ref)
        block = block_rows(place_ref, "part", j, matrix_ref.shape[0] // 27)
        part = lax.dot_general(
            taps,
            tap_rows(moved_ref, block, plane, slots),
            (((0,), (0,)), ((), ())),
            preferred_element_type=jnp.float32,
        )
        if j == 0:
            sum_ref[...] = part if start is None else start + part
        else:
            sum_ref[...] += part


def third(matrix_ref, a):
    rows = matrix_ref.shape[0] // 3
    return matrix_ref[a * rows : (a + 1) * rows]


def middle_kernel(place_ref, grad_ref, *refs):
    matrices, (sum_ref, moved_ref) = refs[:GROUP], refs[GROUP:]
    fill_plane(moved_ref, 0, grad_ref[...])
    add_taps(place_ref, sum_ref, moved_ref, matrices, (0,), lambda ref: third(ref, 1))


def input_kernel(place_ref, middle_ref, low_ref, high_ref, *refs, last):
    matrices, outs = refs[:GROUP], refs[GROUP : GROUP + 7]
    moved_ref, sum_ref = refs[GROUP + 7 :]
    fill_sides(place_ref, moved_ref, (0, 1), low_ref, high_ref, last)

    def sides(ref):
        return jnp.concatenate([third(ref, 0), third(ref, 2)], axis=0)

    add_taps(place_ref, sum_ref, moved_ref, matrices, (1, 0), sides, middle_ref[...])
    half = outs[1].shape[0]
    for out_ref, (j, start) in zip(outs, INPUT_CUTS):
        start = partner(place_ref, "run", j) * 2 * half + start * half
        block = pl.ds(pl.multiple_of(start, half), out_ref.shape[0])
        out_ref[...] = sum_ref[block, :].astype(out_ref.dtype)


INPUT_CUTS = ((0, 0), (2, 0), (2, 1), (1, 0), (3, 1), (1, 1), (3, 0))


def join_kernel(place_ref, near_ref, other_ref, high_ref, low_ref, near_out, other_out):
    del place_ref
    near_out[...] = (near_ref[...] + high_ref[...].astype(jnp.float32)).astype(near_out.dtype)
    other_out[...] = (other_ref[...] + low_ref[...].astype(jnp.float32)).astype(other_out.dtype)


def lift_kernel(place_ref, value_ref, other_ref, out_ref):
    del place_ref
    total = value_ref[...].astype(jnp.float32) + other_ref[...].astype(jnp.float32)
    out_ref[...] = total.astype(out_ref.dtype)


def merge_kernel(place_ref, *refs):
    del place_ref
    values, out_ref = refs[:-1], refs[-1]
    total = values[0][...].astype(jnp.float32)
    for ref in values[1:]:
        total += ref[...].astype(jnp.float32)
    out_ref[...] = total.astype(out_ref.dtype)


def pair_kernel(place_ref, own_ref, *refs):
    halves, active_ref, outs, sum_ref = refs[:4], refs[4], refs[5 : 5 + GROUP], refs[5 + GROUP]
    half = halves[0].shape[0]
    for k in range(2):
        rows = slice(k * half, (k + 1) * half)
        sum_ref[rows, :] = (
            own_ref[rows, :]
            + halves[k][...].astype(jnp.float32)
            + halves[2 + k][...].astype(jnp.float32)
        )
    for j, out_ref in enumerate(outs):
        block = block_rows(place_ref, "part", j, out_ref.shape[1])
        out_ref[0] = active_ref[block, :]
        out_ref[1] = sum_ref[block, :].astype(out_ref.dtype)


def close_kernel(place_ref, *refs):
    pairs, outs = refs[:GROUP], refs[GROUP:]
    for j, pair_ref in enumerate(pairs):
        for k, out_ref in enumerate(outs):
            channels, _, height, breadth = out_ref.shape
            value = pair_ref[k].astype(jnp.float32).reshape(channels, height, breadth)
            out_ref[:, partner_plane(place_ref, j)] = value.astype(out_ref.dtype)


def total_kernel(place_ref, parts_ref, out_ref, *, scale):
    del place_ref
    total = parts_ref[0].astype(jnp.float32)
    for s in range(1, parts_ref.shape[0]):
        total += parts_ref[s].astype(jnp.float32)
    out_ref[...] = jnp.transpose(total * scale)


DEPTH = ("space", "part")
CHANNELS = ("run", "part")


def shifted(value, by):
    count = lax.axis_size(DEPTH)
    at = {
        space * GROUP + plane_of(space, part): space * GROUP + part
        for space in range(count // GROUP)
        for part in range(GROUP)
    }
    return lax.ppermute(value, DEPTH, [(at[i], at[(i + by) % count]) for i in range(count)])


def swap(value, axis, j):
    return lax.ppermute(value, axis, [(i, i ^ j) for i in range(lax.axis_size(axis))])


def swapped(values, axis):
    return [values[0]] + [swap(values[j], axis, j) for j in range(1, GROUP)]


def body(volume, weight, cotangent):
    batch, in_local, planes, height, breadth = volume.shape
    out_local, in_total = weight.shape[3:]
    spaces = lax.axis_size("space")
    plane = height * breadth
    rows, depth, taps = GROUP * out_local, GROUP * in_local, 27 * out_local
    half = depth // 2
    grad_scale = 1.0 / math.sqrt(batch * planes * plane * spaces)
    bf16, f32 = jnp.bfloat16, jnp.float32
    place = lax.axis_index(("space", "run", "part")).reshape(1)
    ends = {"last": spaces - 1}

    volumes = call(
        planes_kernel, [((in_local, plane), bf16)] * GROUP, "volume_planes", place, volume[0]
    )
    matrix, *cotangents = call(
        rest_kernel,
        [((taps, in_total), bf16)] + [((out_local, plane), bf16)] * GROUP,
        "rest",
        place,
        cotangent[0],
        weight.reshape(taps, in_total),
        unread=[volumes[0]],
    )
    volumes, cotangents = swapped(volumes, "part"), swapped(cotangents, "part")
    (block,) = call(
        order_kernel, [((depth, plane), bf16)], "order", place, *volumes, unread=[matrix]
    )
    block_1, block_3 = swap(block, "run", 1), swap(block, "run", 3)
    low_2, high_2 = call(
        cut_kernel, [((half, plane), bf16)] * 2, "cut", place, block_1, block_3
    )
    low_2, high_2 = swap(low_2, "run", 3), swap(high_2, "run", 1)
    matrices = swapped([matrix] * GROUP, "part")

    field, after = call(
        after_kernel,
        [((in_total, plane), bf16), ((rows, plane), bf16)],
        "after",
        place,
        *(block, block_1, block_3, low_2, high_2),
        *matrices,
    )
    after = shifted(after, 1)
    (before,) = call(
        before_kernel,
        [((rows, plane), bf16)],
        "before",
        place,
        field,
        *matrices,
        unread=cotangents[1:],
    )
    (same,) = call(
        centre_kernel,
        [((rows, plane), f32)],
        "centre",
        place,
        field,
        *matrices,
        unread=[before],
    )
    before = shifted(before, -1)
    active, grad = call(
        functools.partial(gate_kernel, **ends),
        [((rows, plane), bf16)] * 2,
        "gate",
        place,
        same,
        before,
        after,
        *cotangents,
    )

    sides = (shifted(grad, 1), shifted(grad, -1))

    def moved(planes):
        return pltpu.VMEM((3, rows, planes * (plane + 2 * BREADTH)), bf16)

    (middle,) = call(
        middle_kernel,
        [((in_total, plane), f32)],
        "middle",
        place,
        grad,
        *matrices,
        scratch=[moved(1)],
        flops=2 * 9 * rows * in_total * plane,
    )
    sums, sums_1, sums_2, sums_3 = call(
        functools.partial(filter_kernel, **ends),
        [((in_total, taps), bf16)] * GROUP,
        "filter_sums",
        place,
        field,
        grad,
        *sides,
        unread=[middle],
        scratch=[moved(3)],
    )
    sums_3, sums_1 = swap(sums_3, "part", 1), swap(sums_1, "part", 1)
    own, far_low, far_high, low_1, high_3, high_1, low_3 = call(
        functools.partial(input_kernel, **ends),
        [((depth, plane), f32)] + [((half, plane), bf16)] * 4 + [((half, plane), f32)] * 2,
        "input_sums",
        place,
        middle,
        *sides,
        *matrices,
        unread=[sums],
        scratch=[moved(2), pltpu.VMEM((in_total, plane), f32)],
    )
    far_low, far_high = swap(far_low, "run", 1), swap(far_high, "run", 3)
    low_1, high_3 = swap(low_1, "run", 1), swap(high_3, "run", 3)
    (sums_2,) = call(
        lift_kernel, [((in_total, taps), bf16)], "lift", place, sums_2, sums_3, unread=[own, sums_1]
    )
    high_1, low_3 = call(
        join_kernel,
        [((half, plane), bf16)] * 2,
        "join",
        place,
        high_1,
        low_3,
        far_high,
        far_low,
        unread=[sums_2],
    )
    high_1, low_3 = swap(high_1, "run", 1), swap(low_3, "run", 3)
    sums_2 = swap(sums_2, "part", 2)
    (sums,) = call(
        merge_kernel,
        [((in_total, taps), bf16)],
        "merge",
        place,
        *(sums, sums_1, sums_2),
        unread=[low_1, high_1, low_3, high_3],
    )
    sums = lax.all_to_all(
        sums.reshape(spaces, in_total // spaces, taps),
        "space",
        split_axis=0,
        concat_axis=0,
        tiled=True,
    )
    pairs = call(
        pair_kernel,
        [((2, in_local, plane), bf16)] * GROUP,
        "pairs",
        place,
        *(own, low_1, high_1, low_3, high_3),
        active,
        scratch=[pltpu.VMEM((depth, plane), f32)],
    )
    pairs = swapped(pairs, "part")
    (total,) = call(
        functools.partial(total_kernel, scale=grad_scale),
        [((taps, in_total // spaces), f32)],
        "total",
        place,
        sums,
    )
    active, back = call(
        close_kernel,
        [((in_local, planes, height, breadth), bf16)] * 2,
        "close",
        place,
        *pairs,
    )
    return (
        active[None],
        back[None],
        total.reshape(3, 3, 3, out_local, in_total // spaces),
    )


def solution(mesh):
    spaces, filts = mesh.devices.shape
    cut = Mesh(mesh.devices.reshape(spaces, filts // GROUP, GROUP), ("space", "run", "part"))
    in_specs = (
        P(None, CHANNELS, "space", None, None),
        P(None, None, None, CHANNELS, None),
        P(None, CHANNELS, "space", None, None),
    )
    out_specs = (
        P(None, CHANNELS, "space", None, None),
        P(None, CHANNELS, "space", None, None),
        P(None, None, None, CHANNELS, "space"),
    )
    return jax.shard_map(body, mesh=cut, in_specs=in_specs, out_specs=out_specs, check_vma=False)
```

```python
import functools
import math

import jax
import jax.numpy as jnp
from jax import lax
from jax.experimental import pallas as pl
from jax.experimental.pallas import tpu as pltpu
from jax.sharding import Mesh, PartitionSpec as P

BREADTH = 128
GROUP = 4
LAYERS = 8
VMEM_LIMIT = 40 * 1024 * 1024


def lane_shifted(value, by):
    if by == 0:
        return value
    lanes = value.shape[1]
    column = lax.broadcasted_iota(jnp.int32, value.shape, 1) % BREADTH
    moved = pltpu.roll(value, (-by) % lanes, 1)
    return jnp.where(column == (BREADTH - 1 if by > 0 else 0), 0.0, moved)


def row_shifted(value, by):
    if by == 0:
        return value
    gap = jnp.zeros((value.shape[0], BREADTH), value.dtype)
    if by > 0:
        return jnp.concatenate([value[:, BREADTH:], gap], axis=1)
    return jnp.concatenate([gap, value[:, :-BREADTH]], axis=1)


def folded(product, channels):
    total = None
    for c in range(3):
        column = None
        for b in range(3):
            at = (b * 3 + c) * channels
            part = row_shifted(product[at : at + channels], b - 1)
            column = part if column is None else column + part
        column = lane_shifted(column, c - 1)
        total = column if total is None else total + column
    return total


def partner(place_ref, axis, j):
    step = {"part": 1, "run": GROUP}[axis]
    return ((place_ref[0] // step) % GROUP) ^ j


def plane_of(space, part):
    backwards = (1 + space + space // LAYERS) % 2
    return part ^ (part // 2) ^ (backwards * (GROUP - 1))


def partner_plane(place_ref, j):
    return plane_of(place_ref[0] // GROUP**2, (place_ref[0] % GROUP) ^ j)


def at_end(place_ref, last):
    space, plane = place_ref[0] // GROUP**2, partner_plane(place_ref, 0)
    if last is None:
        return (space == 0) & (plane == 0)
    return (space == last) & (plane == GROUP - 1)


def unless(condition, value):
    return jnp.where(condition, jnp.zeros_like(value), value)


def block_rows(place_ref, axis, j, rows):
    return pl.ds(pl.multiple_of(partner(place_ref, axis, j) * rows, rows), rows)


def call(kernel, outputs, name, place, *operands, unread=(), scratch=(), flops=1):
    def run(place_ref, *refs):
        kernel(place_ref, *refs[: len(operands)], *refs[len(operands) + len(unread) :])

    return pl.pallas_call(
        run,
        in_specs=[pl.BlockSpec(memory_space=pltpu.SMEM)]
        + [pl.BlockSpec(memory_space=pltpu.VMEM)] * len(operands)
        + [pl.BlockSpec(memory_space=pl.ANY)] * len(unread),
        out_specs=[pl.BlockSpec(memory_space=pltpu.VMEM)] * len(outputs),
        out_shape=[jax.ShapeDtypeStruct(shape, dtype) for shape, dtype in outputs],
        scratch_shapes=list(scratch),
        compiler_params=pltpu.CompilerParams(vmem_limit_bytes=VMEM_LIMIT),
        cost_estimate=pl.CostEstimate(flops=flops, bytes_accessed=1, transcendentals=0),
        name=name,
    )(place, *operands, *unread)


def planes_kernel(place_ref, value_ref, *outs):
    channels, _, height, breadth = value_ref.shape
    for j, out_ref in enumerate(outs):
        value = value_ref[:, partner_plane(place_ref, j)].astype(jnp.float32)
        out_ref[...] = value.reshape(channels, height * breadth).astype(out_ref.dtype)


def rest_kernel(place_ref, cotangent_ref, filters_ref, matrix_ref, *outs):
    planes_kernel(place_ref, cotangent_ref, *outs)
    matrix_ref[...] = filters_ref[...]


def order_kernel(place_ref, *refs):
    pieces, (out_ref,) = refs[:GROUP], refs[GROUP:]
    for j, piece_ref in enumerate(pieces):
        out_ref[block_rows(place_ref, "part", j, piece_ref.shape[0]), :] = piece_ref[...]


def cut_kernel(place_ref, near_ref, other_ref, low_ref, high_ref):
    del place_ref
    half = low_ref.shape[0]
    low_ref[...] = near_ref[:half]
    high_ref[...] = other_ref[half:]


def edge_sums(place_ref, field_ref, matrices, out_ref, a):
    channels = out_ref.shape[0] // GROUP
    rows = 9 * channels
    for j, matrix_ref in enumerate(matrices):
        product = jnp.dot(
            matrix_ref[a * rows : (a + 1) * rows],
            field_ref[...],
            preferred_element_type=jnp.float32,
        )
        block = block_rows(place_ref, "part", j, channels)
        out_ref[block, :] = folded(product, channels).astype(out_ref.dtype)


def after_kernel(place_ref, *refs):
    blocks, halves, matrices = refs[:3], refs[3:5], refs[5 : 5 + GROUP]
    field_ref, after_ref = refs[5 + GROUP :]
    for j, ref in zip((0, 1, 3), blocks):
        field_ref[block_rows(place_ref, "run", j, ref.shape[0]), :] = ref[...]
    for k, ref in enumerate(halves):
        half = ref.shape[0]
        start = (partner(place_ref, "run", 2) * 2 + k) * half
        field_ref[pl.ds(pl.multiple_of(start, half), half), :] = ref[...]
    edge_sums(place_ref, field_ref, matrices, after_ref, 0)


def before_kernel(place_ref, field_ref, *refs):
    edge_sums(place_ref, field_ref, refs[:GROUP], refs[GROUP], 2)


def centre_kernel(place_ref, field_ref, *refs):
    edge_sums(place_ref, field_ref, refs[:GROUP], refs[GROUP], 1)


def gate_kernel(place_ref, same_ref, before_ref, after_ref, *refs, last):
    cotangents, active_ref, grad_ref = refs[:GROUP], refs[GROUP], refs[GROUP + 1]
    channels = cotangents[0].shape[0]
    for j, cotangent_ref in enumerate(cotangents):
        block = block_rows(place_ref, "part", j, channels)
        pre = (
            same_ref[block, :]
            + unless(at_end(place_ref, last), before_ref[block, :].astype(jnp.float32))
            + unless(at_end(place_ref, None), after_ref[block, :].astype(jnp.float32))
        )
        sigma = jax.nn.sigmoid(pre)
        active_ref[block, :] = (pre * sigma).astype(active_ref.dtype)
        grad_ref[block, :] = (
            cotangent_ref[...].astype(jnp.float32) * sigma * (1.0 + pre * (1.0 - sigma))
        ).astype(grad_ref.dtype)


def fill_plane(moved_ref, p, source):
    rows, plane = source.shape
    start = p * (plane + 2 * BREADTH)
    gap = jnp.zeros((rows, BREADTH), moved_ref.dtype)
    source = source.astype(jnp.float32)
    for c in range(3):
        moved_ref[c, :, start : start + BREADTH] = gap
        moved_ref[c, :, start + BREADTH : start + BREADTH + plane] = lane_shifted(
            source, 1 - c
        ).astype(moved_ref.dtype)
        moved_ref[c, :, start + BREADTH + plane : start + 2 * BREADTH + plane] = gap


def fill_sides(place_ref, moved_ref, slots, low_ref, high_ref, last):
    fill_plane(moved_ref, slots[0], unless(at_end(place_ref, None), low_ref[...]))
    fill_plane(moved_ref, slots[1], unless(at_end(place_ref, last), high_ref[...]))


def tap_rows(moved_ref, block, plane, slots):
    parts = []
    for p in slots:
        for b in range(3):
            for c in range(3):
                at = p * (plane + 2 * BREADTH) + (2 - b) * BREADTH
                parts.append(moved_ref[c, block, at : at + plane])
    return jnp.concatenate(parts, axis=0)


def filter_kernel(place_ref, field_ref, grad_ref, low_ref, high_ref, *refs, last):
    outs, moved_ref = refs[:GROUP], refs[GROUP]
    rows, plane = grad_ref.shape
    fill_plane(moved_ref, 1, grad_ref[...])
    fill_sides(place_ref, moved_ref, (0, 2), low_ref, high_ref, last)
    for j, out_ref in enumerate(outs):
        block = block_rows(place_ref, "part", j, rows // GROUP)
        sums = lax.dot_general(
            field_ref[...],
            tap_rows(moved_ref, block, plane, (2, 1, 0)),
            (((1,), (1,)), ((), ())),
            preferred_element_type=jnp.float32,
        )
        out_ref[...] = sums.astype(out_ref.dtype)


def add_taps(place_ref, sum_ref, moved_ref, matrices, slots, pick, start=None):
    plane = sum_ref.shape[1]
    for j, matrix_ref in enumerate(matrices):
        taps = pick(matrix_ref)
        block = block_rows(place_ref, "part", j, matrix_ref.shape[0] // 27)
        part = lax.dot_general(
            taps,
            tap_rows(moved_ref, block, plane, slots),
            (((0,), (0,)), ((), ())),
            preferred_element_type=jnp.float32,
        )
        if j == 0:
            sum_ref[...] = part if start is None else start + part
        else:
            sum_ref[...] += part


def third(matrix_ref, a):
    rows = matrix_ref.shape[0] // 3
    return matrix_ref[a * rows : (a + 1) * rows]


def middle_kernel(place_ref, grad_ref, active_ref, *refs):
    matrices, sum_ref, actives = refs[:GROUP], refs[GROUP], refs[GROUP + 1 : 2 * GROUP + 1]
    moved_ref = refs[2 * GROUP + 1]
    for j, out_ref in enumerate(actives):
        out_ref[...] = active_ref[block_rows(place_ref, "part", j, out_ref.shape[0]), :]
    fill_plane(moved_ref, 0, grad_ref[...])
    add_taps(place_ref, sum_ref, moved_ref, matrices, (0,), lambda ref: third(ref, 1))


def input_kernel(place_ref, middle_ref, low_ref, high_ref, *refs, last):
    matrices, outs = refs[:GROUP], refs[GROUP : GROUP + 7]
    moved_ref, sum_ref = refs[GROUP + 7 :]
    fill_sides(place_ref, moved_ref, (0, 1), low_ref, high_ref, last)

    def sides(ref):
        return jnp.concatenate([third(ref, 0), third(ref, 2)], axis=0)

    add_taps(place_ref, sum_ref, moved_ref, matrices, (1, 0), sides, middle_ref[...])
    half = outs[1].shape[0]
    for out_ref, (j, start) in zip(outs, INPUT_CUTS):
        start = partner(place_ref, "run", j) * 2 * half + start * half
        block = pl.ds(pl.multiple_of(start, half), out_ref.shape[0])
        out_ref[...] = sum_ref[block, :].astype(out_ref.dtype)


INPUT_CUTS = ((0, 0), (2, 0), (2, 1), (1, 0), (3, 1), (1, 1), (3, 0))


def join_kernel(place_ref, near_ref, other_ref, high_ref, low_ref, near_out, other_out):
    del place_ref
    near_out[...] = (near_ref[...] + high_ref[...].astype(jnp.float32)).astype(near_out.dtype)
    other_out[...] = (other_ref[...] + low_ref[...].astype(jnp.float32)).astype(other_out.dtype)


def lift_kernel(place_ref, value_ref, other_ref, out_ref):
    del place_ref
    total = value_ref[...].astype(jnp.float32) + other_ref[...].astype(jnp.float32)
    out_ref[...] = total.astype(out_ref.dtype)


def merge_kernel(place_ref, *refs):
    del place_ref
    values, out_ref = refs[:-1], refs[-1]
    total = values[0][...].astype(jnp.float32)
    for ref in values[1:]:
        total += ref[...].astype(jnp.float32)
    out_ref[...] = total.astype(out_ref.dtype)


def pair_kernel(place_ref, own_ref, *refs):
    halves, outs, sum_ref = refs[:4], refs[4 : 4 + GROUP], refs[4 + GROUP]
    half = halves[0].shape[0]
    for k in range(2):
        rows = slice(k * half, (k + 1) * half)
        sum_ref[rows, :] = (
            own_ref[rows, :]
            + halves[k][...].astype(jnp.float32)
            + halves[2 + k][...].astype(jnp.float32)
        )
    for j, out_ref in enumerate(outs):
        block = block_rows(place_ref, "part", j, out_ref.shape[0])
        out_ref[...] = sum_ref[block, :].astype(out_ref.dtype)


def close_kernel(place_ref, *refs):
    pieces, outs = refs[: 2 * GROUP], refs[2 * GROUP :]
    for k, out_ref in enumerate(outs):
        channels, _, height, breadth = out_ref.shape
        for j in range(GROUP):
            value = pieces[k * GROUP + j][...].astype(jnp.float32)
            out_ref[:, partner_plane(place_ref, j)] = value.reshape(
                channels, height, breadth
            ).astype(out_ref.dtype)


def total_kernel(place_ref, parts_ref, out_ref, *, scale):
    del place_ref
    total = parts_ref[0].astype(jnp.float32)
    for s in range(1, parts_ref.shape[0]):
        total += parts_ref[s].astype(jnp.float32)
    out_ref[...] = jnp.transpose(total * scale)


DEPTH = ("space", "part")
CHANNELS = ("run", "part")


def shifted(value, by):
    count = lax.axis_size(DEPTH)
    at = {
        space * GROUP + plane_of(space, part): space * GROUP + part
        for space in range(count // GROUP)
        for part in range(GROUP)
    }
    return lax.ppermute(value, DEPTH, [(at[i], at[(i + by) % count]) for i in range(count)])


def swap(value, axis, j):
    return lax.ppermute(value, axis, [(i, i ^ j) for i in range(lax.axis_size(axis))])


def swapped(values, axis):
    return [values[0]] + [swap(values[j], axis, j) for j in range(1, GROUP)]


def body(volume, weight, cotangent):
    batch, in_local, planes, height, breadth = volume.shape
    out_local, in_total = weight.shape[3:]
    spaces = lax.axis_size("space")
    plane = height * breadth
    rows, depth, taps = GROUP * out_local, GROUP * in_local, 27 * out_local
    half = depth // 2
    grad_scale = 1.0 / math.sqrt(batch * planes * plane * spaces)
    bf16, f32 = jnp.bfloat16, jnp.float32
    place = lax.axis_index(("space", "run", "part")).reshape(1)
    ends = {"last": spaces - 1}

    volumes = call(
        planes_kernel, [((in_local, plane), bf16)] * GROUP, "volume_planes", place, volume[0]
    )
    matrix, *cotangents = call(
        rest_kernel,
        [((taps, in_total), bf16)] + [((out_local, plane), bf16)] * GROUP,
        "rest",
        place,
        cotangent[0],
        weight.reshape(taps, in_total),
        unread=[volumes[0]],
    )
    volumes, cotangents = swapped(volumes, "part"), swapped(cotangents, "part")
    (block,) = call(
        order_kernel, [((depth, plane), bf16)], "order", place, *volumes, unread=[matrix]
    )
    block_1, block_3 = swap(block, "run", 1), swap(block, "run", 3)
    low_2, high_2 = call(
        cut_kernel, [((half, plane), bf16)] * 2, "cut", place, block_1, block_3
    )
    low_2, high_2 = swap(low_2, "run", 3), swap(high_2, "run", 1)
    matrices = swapped([matrix] * GROUP, "part")

    field, after = call(
        after_kernel,
        [((in_total, plane), bf16), ((rows, plane), bf16)],
        "after",
        place,
        *(block, block_1, block_3, low_2, high_2),
        *matrices,
    )
    after = shifted(after, 1)
    (before,) = call(
        before_kernel,
        [((rows, plane), bf16)],
        "before",
        place,
        field,
        *matrices,
        unread=cotangents[1:],
    )
    (same,) = call(
        centre_kernel,
        [((rows, plane), f32)],
        "centre",
        place,
        field,
        *matrices,
        unread=[before],
    )
    before = shifted(before, -1)
    active, grad = call(
        functools.partial(gate_kernel, **ends),
        [((rows, plane), bf16)] * 2,
        "gate",
        place,
        same,
        before,
        after,
        *cotangents,
    )

    sides = (shifted(grad, 1), shifted(grad, -1))

    def moved(planes):
        return pltpu.VMEM((3, rows, planes * (plane + 2 * BREADTH)), bf16)

    middle, *actives = call(
        middle_kernel,
        [((in_total, plane), f32)] + [((out_local, plane), bf16)] * GROUP,
        "middle",
        place,
        grad,
        active,
        *matrices,
        scratch=[moved(1)],
        flops=2 * 9 * rows * in_total * plane,
    )
    actives = swapped(actives, "part")
    sums, sums_1, sums_2, sums_3 = call(
        functools.partial(filter_kernel, **ends),
        [((in_total, taps), bf16)] * GROUP,
        "filter_sums",
        place,
        field,
        grad,
        *sides,
        unread=[middle, *actives[1:]],
        scratch=[moved(3)],
    )
    sums_3, sums_1 = swap(sums_3, "part", 1), swap(sums_1, "part", 1)
    own, far_low, far_high, low_1, high_3, high_1, low_3 = call(
        functools.partial(input_kernel, **ends),
        [((depth, plane), f32)] + [((half, plane), bf16)] * 4 + [((half, plane), f32)] * 2,
        "input_sums",
        place,
        middle,
        *sides,
        *matrices,
        unread=[sums],
        scratch=[moved(2), pltpu.VMEM((in_total, plane), f32)],
    )
    far_low, far_high = swap(far_low, "run", 1), swap(far_high, "run", 3)
    low_1, high_3 = swap(low_1, "run", 1), swap(high_3, "run", 3)
    (sums_2,) = call(
        lift_kernel, [((in_total, taps), bf16)], "lift", place, sums_2, sums_3, unread=[own, sums_1]
    )
    high_1, low_3 = call(
        join_kernel,
        [((half, plane), bf16)] * 2,
        "join",
        place,
        high_1,
        low_3,
        far_high,
        far_low,
        unread=[sums_2],
    )
    high_1, low_3 = swap(high_1, "run", 1), swap(low_3, "run", 3)
    sums_2 = swap(sums_2, "part", 2)
    (sums,) = call(
        merge_kernel,
        [((in_total, taps), bf16)],
        "merge",
        place,
        *(sums, sums_1, sums_2),
        unread=[low_1, high_1, low_3, high_3],
    )
    sums = lax.all_to_all(
        sums.reshape(spaces, in_total // spaces, taps),
        "space",
        split_axis=0,
        concat_axis=0,
        tiled=True,
    )
    pairs = call(
        pair_kernel,
        [((in_local, plane), bf16)] * GROUP,
        "pairs",
        place,
        *(own, low_1, high_1, low_3, high_3),
        scratch=[pltpu.VMEM((depth, plane), f32)],
    )
    pairs = swapped(pairs, "part")
    (total,) = call(
        functools.partial(total_kernel, scale=grad_scale),
        [((taps, in_total // spaces), f32)],
        "total",
        place,
        sums,
    )
    active, back = call(
        close_kernel,
        [((in_local, planes, height, breadth), bf16)] * 2,
        "close",
        place,
        *actives,
        *pairs,
    )
    return (
        active[None],
        back[None],
        total.reshape(3, 3, 3, out_local, in_total // spaces),
    )


def solution(mesh):
    spaces, filts = mesh.devices.shape
    cut = Mesh(mesh.devices.reshape(spaces, filts // GROUP, GROUP), ("space", "run", "part"))
    in_specs = (
        P(None, CHANNELS, "space", None, None),
        P(None, None, None, CHANNELS, None),
        P(None, CHANNELS, "space", None, None),
    )
    out_specs = (
        P(None, CHANNELS, "space", None, None),
        P(None, CHANNELS, "space", None, None),
        P(None, None, None, CHANNELS, "space"),
    )
    return jax.shard_map(body, mesh=cut, in_specs=in_specs, out_specs=out_specs, check_vma=False)
```

```python
import functools
import math

import jax
import jax.numpy as jnp
from jax import lax
from jax.experimental import pallas as pl
from jax.experimental.pallas import tpu as pltpu
from jax.sharding import Mesh, PartitionSpec as P

BREADTH = 128
GROUP = 4
LAYERS = 8
VMEM_LIMIT = 40 * 1024 * 1024


def lane_shifted(value, by):
    if by == 0:
        return value
    lanes = value.shape[1]
    column = lax.broadcasted_iota(jnp.int32, value.shape, 1) % BREADTH
    moved = pltpu.roll(value, (-by) % lanes, 1)
    return jnp.where(column == (BREADTH - 1 if by > 0 else 0), 0.0, moved)


def row_shifted(value, by):
    if by == 0:
        return value
    gap = jnp.zeros((value.shape[0], BREADTH), value.dtype)
    if by > 0:
        return jnp.concatenate([value[:, BREADTH:], gap], axis=1)
    return jnp.concatenate([gap, value[:, :-BREADTH]], axis=1)


def folded(product, channels):
    total = None
    for c in range(3):
        column = None
        for b in range(3):
            at = (b * 3 + c) * channels
            part = row_shifted(product[at : at + channels], b - 1)
            column = part if column is None else column + part
        column = lane_shifted(column, c - 1)
        total = column if total is None else total + column
    return total


def partner(place_ref, axis, j):
    step = {"part": 1, "run": GROUP}[axis]
    return ((place_ref[0] // step) % GROUP) ^ j


def plane_of(space, part):
    backwards = (1 + space + space // LAYERS) % 2
    return part ^ (part // 2) ^ (backwards * (GROUP - 1))


def partner_plane(place_ref, j):
    return plane_of(place_ref[0] // GROUP**2, (place_ref[0] % GROUP) ^ j)


def at_end(place_ref, last):
    space, plane = place_ref[0] // GROUP**2, partner_plane(place_ref, 0)
    if last is None:
        return (space == 0) & (plane == 0)
    return (space == last) & (plane == GROUP - 1)


def unless(condition, value):
    return jnp.where(condition, jnp.zeros_like(value), value)


def block_rows(place_ref, axis, j, rows):
    return pl.ds(pl.multiple_of(partner(place_ref, axis, j) * rows, rows), rows)


def call(kernel, outputs, name, place, *operands, unread=(), scratch=(), flops=1):
    def run(place_ref, *refs):
        kernel(place_ref, *refs[: len(operands)], *refs[len(operands) + len(unread) :])

    return pl.pallas_call(
        run,
        in_specs=[pl.BlockSpec(memory_space=pltpu.SMEM)]
        + [pl.BlockSpec(memory_space=pltpu.VMEM)] * len(operands)
        + [pl.BlockSpec(memory_space=pl.ANY)] * len(unread),
        out_specs=[pl.BlockSpec(memory_space=pltpu.VMEM)] * len(outputs),
        out_shape=[jax.ShapeDtypeStruct(shape, dtype) for shape, dtype in outputs],
        scratch_shapes=list(scratch),
        compiler_params=pltpu.CompilerParams(vmem_limit_bytes=VMEM_LIMIT),
        cost_estimate=pl.CostEstimate(flops=flops, bytes_accessed=1, transcendentals=0),
        name=name,
    )(place, *operands, *unread)


def planes_kernel(place_ref, value_ref, *outs):
    channels, _, height, breadth = value_ref.shape
    for j, out_ref in enumerate(outs):
        value = value_ref[:, partner_plane(place_ref, j)].astype(jnp.float32)
        out_ref[...] = value.reshape(channels, height * breadth).astype(out_ref.dtype)


def rest_kernel(place_ref, cotangent_ref, filters_ref, matrix_ref, *outs):
    planes_kernel(place_ref, cotangent_ref, *outs)
    matrix_ref[...] = filters_ref[...]


def order_kernel(place_ref, *refs):
    pieces, (out_ref,) = refs[:GROUP], refs[GROUP:]
    for j, piece_ref in enumerate(pieces):
        out_ref[block_rows(place_ref, "part", j, piece_ref.shape[0]), :] = piece_ref[...]


def cut_kernel(place_ref, near_ref, other_ref, low_ref, high_ref):
    del place_ref
    half = low_ref.shape[0]
    low_ref[...] = near_ref[:half]
    high_ref[...] = other_ref[half:]


def edge_sums(place_ref, field_ref, matrices, out_ref, a):
    channels = out_ref.shape[0] // GROUP
    rows = 9 * channels
    for j, matrix_ref in enumerate(matrices):
        product = jnp.dot(
            matrix_ref[a * rows : (a + 1) * rows],
            field_ref[...],
            preferred_element_type=jnp.float32,
        )
        block = block_rows(place_ref, "part", j, channels)
        out_ref[block, :] = folded(product, channels).astype(out_ref.dtype)


def after_kernel(place_ref, *refs):
    blocks, halves, matrices = refs[:3], refs[3:5], refs[5 : 5 + GROUP]
    field_ref, after_ref = refs[5 + GROUP :]
    for j, ref in zip((0, 1, 3), blocks):
        field_ref[block_rows(place_ref, "run", j, ref.shape[0]), :] = ref[...]
    for k, ref in enumerate(halves):
        half = ref.shape[0]
        start = (partner(place_ref, "run", 2) * 2 + k) * half
        field_ref[pl.ds(pl.multiple_of(start, half), half), :] = ref[...]
    edge_sums(place_ref, field_ref, matrices, after_ref, 0)


def before_kernel(place_ref, field_ref, *refs):
    edge_sums(place_ref, field_ref, refs[:GROUP], refs[GROUP], 2)


def centre_kernel(place_ref, field_ref, *refs):
    edge_sums(place_ref, field_ref, refs[:GROUP], refs[GROUP], 1)


def gate_kernel(place_ref, same_ref, before_ref, after_ref, *refs, last):
    cotangents, active_ref, grad_ref = refs[:GROUP], refs[GROUP], refs[GROUP + 1]
    channels = cotangents[0].shape[0]
    for j, cotangent_ref in enumerate(cotangents):
        block = block_rows(place_ref, "part", j, channels)
        pre = (
            same_ref[block, :]
            + unless(at_end(place_ref, last), before_ref[block, :].astype(jnp.float32))
            + unless(at_end(place_ref, None), after_ref[block, :].astype(jnp.float32))
        )
        sigma = jax.nn.sigmoid(pre)
        active_ref[block, :] = (pre * sigma).astype(active_ref.dtype)
        grad_ref[block, :] = (
            cotangent_ref[...].astype(jnp.float32) * sigma * (1.0 + pre * (1.0 - sigma))
        ).astype(grad_ref.dtype)


def fill_plane(moved_ref, p, source):
    rows, plane = source.shape
    start = p * (plane + 2 * BREADTH)
    gap = jnp.zeros((rows, BREADTH), moved_ref.dtype)
    source = source.astype(jnp.float32)
    for c in range(3):
        moved_ref[c, :, start : start + BREADTH] = gap
        moved_ref[c, :, start + BREADTH : start + BREADTH + plane] = lane_shifted(
            source, 1 - c
        ).astype(moved_ref.dtype)
        moved_ref[c, :, start + BREADTH + plane : start + 2 * BREADTH + plane] = gap


def fill_sides(place_ref, moved_ref, slots, low_ref, high_ref, last):
    fill_plane(moved_ref, slots[0], unless(at_end(place_ref, None), low_ref[...]))
    fill_plane(moved_ref, slots[1], unless(at_end(place_ref, last), high_ref[...]))


def tap_rows(moved_ref, block, plane, slots):
    parts = []
    for p in slots:
        for b in range(3):
            for c in range(3):
                at = p * (plane + 2 * BREADTH) + (2 - b) * BREADTH
                parts.append(moved_ref[c, block, at : at + plane])
    return jnp.concatenate(parts, axis=0)


def filter_kernel(place_ref, field_ref, grad_ref, low_ref, high_ref, *refs, last):
    outs, moved_ref = refs[:GROUP], refs[GROUP]
    rows, plane = grad_ref.shape
    fill_plane(moved_ref, 1, grad_ref[...])
    fill_sides(place_ref, moved_ref, (0, 2), low_ref, high_ref, last)
    for j, out_ref in enumerate(outs):
        block = block_rows(place_ref, "part", j, rows // GROUP)
        sums = lax.dot_general(
            field_ref[...],
            tap_rows(moved_ref, block, plane, (2, 1, 0)),
            (((1,), (1,)), ((), ())),
            preferred_element_type=jnp.float32,
        )
        out_ref[...] = sums.astype(out_ref.dtype)


def add_taps(place_ref, sum_ref, moved_ref, matrices, slots, pick, start=None):
    plane = sum_ref.shape[1]
    for j, matrix_ref in enumerate(matrices):
        taps = pick(matrix_ref)
        block = block_rows(place_ref, "part", j, matrix_ref.shape[0] // 27)
        part = lax.dot_general(
            taps,
            tap_rows(moved_ref, block, plane, slots),
            (((0,), (0,)), ((), ())),
            preferred_element_type=jnp.float32,
        )
        if j == 0:
            sum_ref[...] = part if start is None else start + part
        else:
            sum_ref[...] += part


def third(matrix_ref, a):
    rows = matrix_ref.shape[0] // 3
    return matrix_ref[a * rows : (a + 1) * rows]


def middle_kernel(place_ref, grad_ref, active_ref, *refs):
    matrices, sum_ref, actives = refs[:GROUP], refs[GROUP], refs[GROUP + 1 : 2 * GROUP + 1]
    moved_ref = refs[2 * GROUP + 1]
    for j, out_ref in enumerate(actives):
        out_ref[...] = active_ref[block_rows(place_ref, "part", j, out_ref.shape[0]), :]
    fill_plane(moved_ref, 0, grad_ref[...])
    add_taps(place_ref, sum_ref, moved_ref, matrices, (0,), lambda ref: third(ref, 1))


def input_kernel(place_ref, middle_ref, low_ref, high_ref, *refs, last):
    matrices, outs = refs[:GROUP], refs[GROUP : GROUP + 7]
    moved_ref, sum_ref = refs[GROUP + 7 :]
    fill_sides(place_ref, moved_ref, (0, 1), low_ref, high_ref, last)

    def sides(ref):
        return jnp.concatenate([third(ref, 0), third(ref, 2)], axis=0)

    add_taps(place_ref, sum_ref, moved_ref, matrices, (1, 0), sides, middle_ref[...])
    half = outs[1].shape[0]
    for out_ref, (j, start) in zip(outs, INPUT_CUTS):
        start = partner(place_ref, "run", j) * 2 * half + start * half
        block = pl.ds(pl.multiple_of(start, half), out_ref.shape[0])
        out_ref[...] = sum_ref[block, :].astype(out_ref.dtype)


INPUT_CUTS = ((0, 0), (2, 0), (2, 1), (1, 0), (3, 1), (1, 1), (3, 0))


def join_kernel(place_ref, near_ref, other_ref, high_ref, low_ref, near_out, other_out):
    del place_ref
    near_out[...] = (near_ref[...] + high_ref[...].astype(jnp.float32)).astype(near_out.dtype)
    other_out[...] = (other_ref[...] + low_ref[...].astype(jnp.float32)).astype(other_out.dtype)


def lift_kernel(place_ref, value_ref, other_ref, out_ref):
    del place_ref
    total = value_ref[...].astype(jnp.float32) + other_ref[...].astype(jnp.float32)
    out_ref[...] = total.astype(out_ref.dtype)


def merge_kernel(place_ref, *refs):
    del place_ref
    values, out_ref = refs[:-1], refs[-1]
    total = values[0][...].astype(jnp.float32)
    for ref in values[1:]:
        total += ref[...].astype(jnp.float32)
    out_ref[...] = total.astype(out_ref.dtype)


def pair_kernel(place_ref, own_ref, *refs):
    halves, outs, sum_ref = refs[:4], refs[4 : 4 + GROUP], refs[4 + GROUP]
    half = halves[0].shape[0]
    for k in range(2):
        rows = slice(k * half, (k + 1) * half)
        sum_ref[rows, :] = (
            own_ref[rows, :]
            + halves[k][...].astype(jnp.float32)
            + halves[2 + k][...].astype(jnp.float32)
        )
    for j, out_ref in enumerate(outs):
        block = block_rows(place_ref, "part", j, out_ref.shape[0])
        out_ref[...] = sum_ref[block, :].astype(out_ref.dtype)


def close_kernel(place_ref, *refs):
    pieces, outs = refs[: 2 * GROUP], refs[2 * GROUP :]
    for k, out_ref in enumerate(outs):
        channels, _, height, breadth = out_ref.shape
        for j in range(GROUP):
            value = pieces[k * GROUP + j][...].astype(jnp.float32)
            out_ref[:, partner_plane(place_ref, j)] = value.reshape(
                channels, height, breadth
            ).astype(out_ref.dtype)


def total_kernel(place_ref, parts_ref, out_ref, *, scale):
    del place_ref
    total = parts_ref[0].astype(jnp.float32)
    for s in range(1, parts_ref.shape[0]):
        total += parts_ref[s].astype(jnp.float32)
    out_ref[...] = jnp.transpose(total * scale)


DEPTH = ("space", "part")
CHANNELS = ("run", "part")


def shifted(value, by):
    count = lax.axis_size(DEPTH)
    at = {
        space * GROUP + plane_of(space, part): space * GROUP + part
        for space in range(count // GROUP)
        for part in range(GROUP)
    }
    return lax.ppermute(value, DEPTH, [(at[i], at[(i + by) % count]) for i in range(count)])


def swap(value, axis, j):
    return lax.ppermute(value, axis, [(i, i ^ j) for i in range(lax.axis_size(axis))])


def swapped(values, axis):
    return [values[0]] + [swap(values[j], axis, j) for j in range(1, GROUP)]


def body(volume, weight, cotangent):
    batch, in_local, planes, height, breadth = volume.shape
    out_local, in_total = weight.shape[3:]
    spaces = lax.axis_size("space")
    plane = height * breadth
    rows, depth, taps = GROUP * out_local, GROUP * in_local, 27 * out_local
    half = depth // 2
    grad_scale = 1.0 / math.sqrt(batch * planes * plane * spaces)
    bf16, f32 = jnp.bfloat16, jnp.float32
    place = lax.axis_index(("space", "run", "part")).reshape(1)
    ends = {"last": spaces - 1}

    volumes = call(
        planes_kernel, [((in_local, plane), bf16)] * GROUP, "volume_planes", place, volume[0]
    )
    matrix, *cotangents = call(
        rest_kernel,
        [((taps, in_total), bf16)] + [((out_local, plane), bf16)] * GROUP,
        "rest",
        place,
        cotangent[0],
        weight.reshape(taps, in_total),
        unread=[volumes[0]],
    )
    volumes, cotangents = swapped(volumes, "part"), swapped(cotangents, "part")
    (block,) = call(
        order_kernel, [((depth, plane), bf16)], "order", place, *volumes, unread=[matrix]
    )
    block_1, block_3 = swap(block, "run", 1), swap(block, "run", 3)
    low_2, high_2 = call(
        cut_kernel, [((half, plane), bf16)] * 2, "cut", place, block_1, block_3
    )
    low_2, high_2 = swap(low_2, "run", 3), swap(high_2, "run", 1)
    matrices = swapped([matrix] * GROUP, "part")

    field, after = call(
        after_kernel,
        [((in_total, plane), bf16), ((rows, plane), bf16)],
        "after",
        place,
        *(block, block_1, block_3, low_2, high_2),
        *matrices,
    )
    after = shifted(after, 1)
    (before,) = call(
        before_kernel,
        [((rows, plane), bf16)],
        "before",
        place,
        field,
        *matrices,
        unread=cotangents[1:],
    )
    (same,) = call(
        centre_kernel,
        [((rows, plane), f32)],
        "centre",
        place,
        field,
        *matrices,
        unread=[before],
    )
    before = shifted(before, -1)
    active, grad = call(
        functools.partial(gate_kernel, **ends),
        [((rows, plane), bf16)] * 2,
        "gate",
        place,
        same,
        before,
        after,
        *cotangents,
    )

    sides = (shifted(grad, 1), shifted(grad, -1))

    def moved(planes):
        return pltpu.VMEM((3, rows, planes * (plane + 2 * BREADTH)), bf16)

    middle, *actives = call(
        middle_kernel,
        [((in_total, plane), f32)] + [((out_local, plane), bf16)] * GROUP,
        "middle",
        place,
        grad,
        active,
        *matrices,
        scratch=[moved(1)],
        flops=2 * 9 * rows * in_total * plane,
    )
    actives = swapped(actives, "part")
    sums, sums_1, sums_2, sums_3 = call(
        functools.partial(filter_kernel, **ends),
        [((in_total, taps), bf16)] * GROUP,
        "filter_sums",
        place,
        field,
        grad,
        *sides,
        unread=[middle],
        scratch=[moved(3)],
    )
    sums_3, sums_1 = swap(sums_3, "part", 1), swap(sums_1, "part", 1)
    own, far_low, far_high, low_1, high_3, high_1, low_3 = call(
        functools.partial(input_kernel, **ends),
        [((depth, plane), f32)] + [((half, plane), bf16)] * 4 + [((half, plane), f32)] * 2,
        "input_sums",
        place,
        middle,
        *sides,
        *matrices,
        unread=[sums, *actives[1:]],
        scratch=[moved(2), pltpu.VMEM((in_total, plane), f32)],
    )
    far_low, far_high = swap(far_low, "run", 1), swap(far_high, "run", 3)
    low_1, high_3 = swap(low_1, "run", 1), swap(high_3, "run", 3)
    (sums_2,) = call(
        lift_kernel, [((in_total, taps), bf16)], "lift", place, sums_2, sums_3, unread=[own, sums_1]
    )
    high_1, low_3 = call(
        join_kernel,
        [((half, plane), bf16)] * 2,
        "join",
        place,
        high_1,
        low_3,
        far_high,
        far_low,
        unread=[sums_2],
    )
    high_1, low_3 = swap(high_1, "run", 1), swap(low_3, "run", 3)
    sums_2 = swap(sums_2, "part", 2)
    (sums,) = call(
        merge_kernel,
        [((in_total, taps), bf16)],
        "merge",
        place,
        *(sums, sums_1, sums_2),
        unread=[low_1, high_1, low_3, high_3],
    )
    sums = lax.all_to_all(
        sums.reshape(spaces, in_total // spaces, taps),
        "space",
        split_axis=0,
        concat_axis=0,
        tiled=True,
    )
    pairs = call(
        pair_kernel,
        [((in_local, plane), bf16)] * GROUP,
        "pairs",
        place,
        *(own, low_1, high_1, low_3, high_3),
        scratch=[pltpu.VMEM((depth, plane), f32)],
    )
    pairs = swapped(pairs, "part")
    (total,) = call(
        functools.partial(total_kernel, scale=grad_scale),
        [((taps, in_total // spaces), f32)],
        "total",
        place,
        sums,
    )
    active, back = call(
        close_kernel,
        [((in_local, planes, height, breadth), bf16)] * 2,
        "close",
        place,
        *actives,
        *pairs,
    )
    return (
        active[None],
        back[None],
        total.reshape(3, 3, 3, out_local, in_total // spaces),
    )


def solution(mesh):
    spaces, filts = mesh.devices.shape
    cut = Mesh(mesh.devices.reshape(spaces, filts // GROUP, GROUP), ("space", "run", "part"))
    in_specs = (
        P(None, CHANNELS, "space", None, None),
        P(None, None, None, CHANNELS, None),
        P(None, CHANNELS, "space", None, None),
    )
    out_specs = (
        P(None, CHANNELS, "space", None, None),
        P(None, CHANNELS, "space", None, None),
        P(None, None, None, CHANNELS, "space"),
    )
    return jax.shard_map(body, mesh=cut, in_specs=in_specs, out_specs=out_specs, check_vma=False)
```
